1024 devices in a mesh: oy: 16 (over y, core), ox: 64 (over x, z).
Axes of the slice: x: 8, y: 8, z: 8, core: 2. Of those that a mesh axis runs over, the one named last changes fastest.
Arguments:
- atm_flux: bfloat16 [4, 16, 49152], P(None, 'oy', 'ox'), may hold values from -6 to 6
- remap_weight: bfloat16 [16, 3584, 128, 128], P('oy', 'ox'), may hold values from -0.5 to 0.5
- source_block: int32 [16, 3584], P('oy', 'ox'), may hold values from 0 to 5
- send_counts: int32 [16, 448], P('oy', 'ox'), may hold values from 4 to 8, as said below
- recv_rows: int32 [16, 3584], P('oy', 'ox'), may hold values from 0 to 15, as said below
- land_mask: int32 [256, 8192], P('oy', 'ox'), may hold values 0 or 1
- tracers: float32 [3, 4, 256, 8192], P(None, None, 'oy', 'ox'), may hold values from -6 to 6
- east_velocity: float32 [4, 256, 8192], P(None, 'oy', 'ox'), may hold values from -0.2 to 0.2
- north_velocity: float32 [4, 256, 8192], P(None, 'oy', 'ox'), may hold values from -0.2 to 0.2
Outputs:
- ocean_flux: float32 [4, 256, 8192], P(None, 'oy', 'ox')
- new_tracers: float32 [3, 4, 256, 8192], P(None, None, 'oy', 'ox')
The draws below stay inside these ranges and needn't reach their ends.
Inputs may be any that keep to these rules, and one draw needn't show every extreme that they name: send_counts[y, x * 7 + g] counts the first slots of group g that are live; every draw has a device that receives 8 live blocks from each of its 7 sources. `recv_rows`: for every receiving device, the slots with c < 4 name every row of its tile.
All inputs are finite; a program needn't handle non-finite values. No bound on the sum of `land_mask` on one device may be relied on, other than what follows from the above.
Results may differ from the reference program's by a relative error of at most 0.015.
Values sent between devices are 32-bit elements; how exact they have to be, the bound alone decides.
A program may use at most 32 MiB of HBM per device.

```python
import jax
import jax.numpy as jnp
from jax import lax

FLUX = 4
TRACERS = 3
LEVELS = 4
STEPS = 2
BA = 128
TX = 128
TY = 16
NB = 6
REACH = 3
CAP = 8
GROUPS = 7
SLOTS = 56
ATM_DEV = 768
NY = 256
NX = 8192
N_OY = 16
N_OX = 64


def draw_send_counts(key, part):
    key = jax.random.fold_in(key, 11)
    first, second, third = jax.random.split(key, 3)
    counts = jax.random.randint(first, (N_OY, N_OX, GROUPS), CAP // 2, CAP + 1)
    row_pick = jax.random.randint(second, (), 0, N_OY)
    column_pick = jax.random.randint(third, (), 0, N_OX)
    group = jnp.arange(GROUPS)
    senders = (column_pick - (group - REACH)) % N_OX
    counts = counts.at[row_pick, senders, group].set(CAP)
    return counts.reshape(N_OY, N_OX * GROUPS).astype(jnp.int32)


def draw_recv_rows(key, part):
    key = jax.random.fold_in(key, 23)
    first, second = jax.random.split(key, 2)
    sure = GROUPS * (CAP // 2)
    scores = jax.random.randint(first, (N_OY, N_OX, sure), 0, 4096)
    scores = scores * sure + jnp.arange(sure)[None, None, :]
    order = jnp.argsort(scores, axis=-1, stable=True).astype(jnp.int32)
    covering = order % TY
    extra = jax.random.randint(second, (N_OY, N_OX, SLOTS), 0, TY)
    slot = jnp.arange(SLOTS)
    low = slot % CAP
    index = (low * GROUPS + slot // CAP) % sure
    picked = covering[:, :, index]
    rows = jnp.where((low < CAP // 2)[None, None, :], picked, extra)
    return rows.reshape(N_OY, N_OX * SLOTS).astype(jnp.int32)


def plant(array, key, least, high):
    dims = array.shape
    place = [jax.random.randint(jax.random.fold_in(key, axis), (), 0, dims[axis]) for axis in range(len(dims))]
    array = array.at[tuple(place)].set(least)
    longest = dims.index(max(dims))
    place[longest] = (place[longest] + 1) % dims[longest]
    return array.at[tuple(place)].set(high)


def levels(own_key, dims, shards, low, high):
    loudness = 1.0
    for axis_at, blocks in shards:
        steps = jax.random.uniform(jax.random.fold_in(jax.random.fold_in(own_key, 6), axis_at), (blocks,), jnp.float32, low / len(shards), high / len(shards))
        loudness = loudness * jnp.repeat(jnp.exp(steps), dims[axis_at] // blocks).reshape((-1,) + (1,) * (len(dims) - 1 - axis_at))
    return loudness


def gaussian(own_key, dims, scale, bound, shards=(), held_as=jnp.bfloat16):
    loudness = levels(own_key, dims, shards, -0.22, 0.18) if shards else 1.0
    array = jax.random.normal(own_key, dims, jnp.float32) * scale * loudness
    return jnp.minimum(jnp.maximum(array, -bound), bound).astype(held_as)


def setup_inputs(seed: int = 0) -> dict:
    seeds = jax.random.split(jax.random.key(seed), 10)
    return {
        "atm_flux": gaussian(seeds[0], (FLUX, N_OY, N_OX * ATM_DEV), 1.0, 6.0, ((1, 16), (2, 64))),
        "remap_weight": gaussian(seeds[1], (N_OY, N_OX * SLOTS, BA, TX), BA ** -0.5, 0.5, ((0, 16), (1, 64))),
        "source_block": plant(jax.random.randint(seeds[2], (N_OY, N_OX * SLOTS), 0, NB), jax.random.fold_in(seeds[2], 1), 0, NB - 1).astype(jnp.int32),
        "send_counts": draw_send_counts(jax.random.fold_in(seeds[9], 71), 0),
        "recv_rows": draw_recv_rows(jax.random.fold_in(seeds[9], 71), 0),
        "land_mask": plant((jax.random.randint(seeds[5], (NY, NX), 0, 5) < 4).astype(jnp.int32), jax.random.fold_in(seeds[5], 1), 0, 1),
        "tracers": gaussian(seeds[6], (TRACERS, LEVELS, NY, NX), 1.0, 6.0, ((2, 16), (3, 64)), jnp.float32),
        "east_velocity": jnp.clip(jax.random.uniform(seeds[7], (LEVELS, NY, NX), jnp.float32, -0.2, 0.2) * levels(seeds[7], (LEVELS, NY, NX), ((1, 16), (2, 64)), -0.4, 0.0), -0.2, 0.2),
        "north_velocity": jnp.clip(jax.random.uniform(seeds[8], (LEVELS, NY, NX), jnp.float32, -0.2, 0.2) * levels(seeds[8], (LEVELS, NY, NX), ((1, 16), (2, 64)), -0.4, 0.0), -0.2, 0.2),
    }


lateral_mixing = 0.08
vertical_mixing = 0.1
surface_gain = 0.5


def neighbours(field):
    lead = [(0, 0)] * (field.ndim - 2)
    padded = jnp.pad(field, lead + [(1, 1), (0, 0)])
    north_side = padded[..., 2:, :]
    south_side = padded[..., :-2, :]
    east_side = jnp.roll(field, -1, axis=-1)
    west_side = jnp.roll(field, 1, axis=-1)
    return east_side, west_side, north_side, south_side


def tendency_step(center, sides, wet, wet_sides, eastward, northward, kv_top, source):
    east_side, west_side, north_side, south_side = sides
    wet_east, wet_west, wet_north, wet_south = wet_sides
    advect = jnp.maximum(eastward, 0.0) * (center - west_side) + jnp.minimum(eastward, 0.0) * (east_side - center)
    advect = advect + jnp.maximum(northward, 0.0) * (center - south_side) + jnp.minimum(northward, 0.0) * (north_side - center)
    spread = lateral_mixing * (wet_east * (east_side - center) + wet_west * (west_side - center)
                               + wet_north * (north_side - center) + wet_south * (south_side - center))
    faces = jnp.concatenate([kv_top[None, None] * (center[:, 1:2] - center[:, 0:1]),
                             vertical_mixing * (center[:, 2:] - center[:, 1:-1])], axis=1)
    zeros = jnp.zeros_like(center[:, :1])
    vdiff = jnp.concatenate([faces, zeros], axis=1) - jnp.concatenate([zeros, faces], axis=1)
    surface = jnp.concatenate([source[:, None], jnp.zeros_like(center[:, 1:])], axis=1)
    return center + wet * (-advect + spread + vdiff + surface)


def reference(atm_flux, remap_weight, source_block, send_counts, recv_rows, land_mask, tracers, east_velocity, north_velocity):
    flux_rows = jnp.moveaxis(atm_flux.reshape(FLUX, N_OY, N_OX, NB, BA), 0, 3)
    weights = remap_weight.reshape(N_OY, N_OX, SLOTS, BA, TX)
    sources = source_block.reshape(N_OY, N_OX, SLOTS)

    def one_row(items):
        blocks, block_weights, chosen = items
        picked = blocks[jnp.arange(N_OX)[:, None], chosen]
        return jnp.einsum('xsfb,xsbc->xsfc', picked.astype(jnp.float32), block_weights.astype(jnp.float32))

    partial_value = lax.map(one_row, (flux_rows, weights, sources))
    slot = jnp.arange(SLOTS)
    counts = send_counts.reshape(N_OY, N_OX, GROUPS)
    live = (slot % CAP)[None, None, :] < counts[:, :, slot // CAP]
    partial_value = partial_value * live[..., None, None].astype(jnp.float32)
    grouped = partial_value.reshape(N_OY, N_OX, GROUPS, CAP, FLUX, TX)
    received = jnp.stack([jnp.roll(grouped[:, :, group], group - REACH, axis=1) for group in range(GROUPS)], axis=2)
    received = received.reshape(N_OY, N_OX, SLOTS, FLUX, TX)
    rows = recv_rows.reshape(N_OY, N_OX, SLOTS)
    onehot = (rows[..., None] == jnp.arange(TY)[None, None, None, :]).astype(jnp.float32)
    tiles = jnp.einsum('yxst,yxsfc->fytxc', onehot, received, precision=lax.Precision.HIGHEST)
    ocean_flux = tiles.reshape(FLUX, NY, NX)

    wet = land_mask.astype(jnp.float32)
    wet_sides = neighbours(wet)
    mixing = ocean_flux[FLUX - 1]
    kv_top = 0.05 + 0.15 * mixing * mixing / (1.0 + mixing * mixing)
    source = surface_gain * ocean_flux[:TRACERS]
    state = tracers
    for step in range(STEPS):
        state = tendency_step(state, neighbours(state), wet, wet_sides, east_velocity[None], north_velocity[None], kv_top, source)
    return ocean_flux, state
```

```python
import jax
import jax.numpy as jnp
from jax import lax
from jax.experimental import pallas as pl
from jax.experimental.pallas import tpu as pltpu
from jax.sharding import PartitionSpec as P

MESH = pl.DeviceIdType.MESH
FLUX = 4
TRACERS = 3
LEVELS = 4
FIELDS = TRACERS * LEVELS
ROWS = 16
COLS = 128
BLOCKS = 6
REACH = 3
CAP = 8
GROUPS = 7
SLOTS = GROUPS * CAP
ORDER = (0, 6, 1, 5, 2, 4, 3)
NEAR = (1, 2, 3, 4, 5)
FAR = (0, 6)
LATERAL = 0.08
VERTICAL = 0.1
GAIN = 0.5
F32 = jnp.float32
BF16 = jnp.bfloat16


def lanes(shape):
    return lax.broadcasted_iota(jnp.int32, shape, len(shape) - 1)


def rows(shape):
    return lax.broadcasted_iota(jnp.int32, shape, len(shape) - 2)


def kernel(
    flux_h, weight_h, source_h, count_h, recv_h, land_h, tracer_h, east_h, north_h,
    ocean_o, new_o,
    flux_v, weight_v, source_v, count_v, place_v, land_v, tracer_v, east_v, north_v,
    lhs_v, send_v, recv_v, state_v, col_out, col_in, row_out, row_in,
    load_sem, weight_sem, part_send, part_recv, halo_send, halo_recv,
):
    oy, ox = lax.axis_index("oy"), lax.axis_index("ox")
    n_oy, n_ox = lax.axis_size("oy"), lax.axis_size("ox")

    def along(offset):
        return (oy, lax.rem(ox + (n_ox + offset), n_ox))

    up = (lax.rem(oy + 1, n_oy), ox)
    down = (lax.rem(oy + (n_oy - 1), n_oy), ox)

    loads = {}
    for i, (name, src, dst) in enumerate((
        ("tracer", tracer_h, tracer_v), ("land", land_h, land_v), ("flux", flux_h, flux_v),
        ("source", source_h, source_v), ("count", count_h, count_v), ("place", recv_h, place_v),
        ("east", east_h, east_v), ("north", north_h, north_v),
    )):
        loads[name] = pltpu.make_async_copy(src, dst, load_sem.at[i])
    weights = {
        g: pltpu.make_async_copy(
            weight_h.at[pl.ds(g * CAP, CAP)], weight_v.at[pl.ds(g * CAP, CAP)], weight_sem.at[g]
        )
        for g in range(GROUPS)
    }
    for name in ("tracer", "land", "flux", "source", "count"):
        loads[name].start()
    for g in ORDER:
        weights[g].start()
    for name in ("place", "east", "north"):
        loads[name].start()

    barrier = pltpu.get_barrier_semaphore()
    partners = [along(d) for d in (-3, 3, -2, 2, -1, 1)] + [up, down]
    for device in partners:
        pl.semaphore_signal(barrier, inc=1, device_id=device, device_id_type=MESH)

    def halo_copies(e):
        out = []
        for side, (src, dst, device) in enumerate((
            (row_out.at[e, 0], row_in.at[e, 0], down), (row_out.at[e, 1], row_in.at[e, 1], up),
            (col_out.at[e], col_in.at[e, 0], along(1)), (col_out.at[e], col_in.at[e, 1], along(-1)),
        )):
            out.append(pltpu.make_async_remote_copy(
                src_ref=src, dst_ref=dst, send_sem=halo_send.at[e, side], recv_sem=halo_recv.at[e, side],
                device_id=device, device_id_type=MESH,
            ))
        return out

    lane = lanes((ROWS, COLS))
    row = rows((ROWS, COLS))

    def pack(fields):
        packed = jnp.zeros((ROWS, COLS), F32)
        for k, field in enumerate(fields):
            packed = jnp.where((lane == 2 * k) | (lane == 2 * k + 1), pltpu.roll(field, 2 * k + 1, 1), packed)
        return packed

    def shift(x, by, axis):
        return pltpu.roll(x, by % x.shape[axis], axis)

    loads["tracer"].wait()
    loads["land"].wait()
    wet = land_v[...].astype(F32)
    first = [tracer_v[pl.ds(k * ROWS, ROWS), :] for k in range(FIELDS)]
    row_out[0, 0, 0:FIELDS, :] = tracer_v[pl.ds(0, FIELDS, stride=ROWS), :]
    row_out[0, 1, 0:FIELDS, :] = tracer_v[pl.ds(ROWS - 1, FIELDS, stride=ROWS), :]
    row_out[0, 0, FIELDS:ROWS, :] = jnp.broadcast_to(wet[0:1], (ROWS - FIELDS, COLS))
    row_out[0, 1, FIELDS:ROWS, :] = jnp.broadcast_to(wet[ROWS - 1 : ROWS], (ROWS - FIELDS, COLS))
    col_out[0] = pack(first + [wet])

    loads["flux"].wait()
    loads["source"].wait()
    loads["count"].wait()
    flux = flux_v[...].astype(F32)
    blocks = jnp.concatenate([flux[:, n * COLS : (n + 1) * COLS] for n in range(BLOCKS)], axis=0)
    blocks = jnp.concatenate([blocks, jnp.zeros((COLS - FLUX * BLOCKS, COLS), F32)], axis=0).astype(BF16)
    wide = FLUX * SLOTS
    at_slot = rows((wide, SLOTS)) // FLUX == lanes((wide, SLOTS))
    at_group = rows((wide, GROUPS)) // (FLUX * CAP) == lanes((wide, GROUPS))
    source = jnp.where(at_slot, source_v[...].astype(F32), 0.0).astype(BF16)
    count = jnp.where(at_group, count_v[...].astype(F32), 0.0).astype(BF16)
    source = jnp.dot(source, jnp.ones((SLOTS, COLS), BF16), preferred_element_type=F32)
    count = jnp.dot(count, jnp.ones((GROUPS, COLS), BF16), preferred_element_type=F32)
    r, c = rows((wide, COLS)), lanes((wide, COLS))
    pick = (
        (source == (c // FLUX).astype(F32))
        & (r % FLUX == c % FLUX)
        & (((r // FLUX) % CAP).astype(F32) < count)
    )
    chosen = jnp.dot(jnp.where(pick, 1.0, 0.0).astype(BF16), blocks, preferred_element_type=F32)
    low = r % 16 < 8
    lhs_v[:, 0:COLS] = jnp.where(low, chosen, 0.0).astype(BF16)
    lhs_v[:, COLS : 2 * COLS] = jnp.where(low, 0.0, chosen).astype(BF16)

    parts = {}
    for g in range(GROUPS):
        if g != REACH:
            parts[g] = pltpu.make_async_remote_copy(
                src_ref=send_v.at[g], dst_ref=recv_v.at[g], send_sem=part_send.at[g],
                recv_sem=part_recv.at[g], device_id=along(g - REACH), device_id_type=MESH,
            )

    half = rows((16, COLS)) % 8 < 4
    halo = halo_copies(0)
    for i, g in enumerate(ORDER):
        weights[g].wait()
        for q in (2 * g, 2 * g + 1):
            w = [weight_v[4 * q + j] for j in range(4)]
            tile = jnp.concatenate(
                [jnp.concatenate(w[0:2], axis=1), jnp.concatenate(w[2:4], axis=1)], axis=0
            )
            both = jnp.dot(lhs_v[pl.ds(16 * q, 16), :], tile, preferred_element_type=F32)
            value = jnp.where(half, both[:, 0:COLS], both[:, COLS:])
            target = recv_v if g == REACH else send_v
            target[g, pl.ds(16 * (q - 2 * g), 16), :] = value
        if i == 0:
            pl.semaphore_wait(barrier, len(partners))
        if g != REACH:
            parts[g].start()
        if i == 1:
            for copy in halo:
                copy.start()

    loads["place"].wait()
    expand = jnp.where(lanes((SLOTS, wide)) // FLUX == rows((SLOTS, wide)), 1.0, 0.0).astype(BF16)
    target_row = jnp.dot(
        jnp.broadcast_to(place_v[...].astype(F32), (8, SLOTS)).astype(BF16), expand, preferred_element_type=F32
    )
    r, c = rows((FLUX * ROWS, wide)), lanes((FLUX * ROWS, wide))
    place = jnp.where(
        (target_row[0:1] == (r % ROWS).astype(F32)) & (c % FLUX == r // ROWS), 1.0, 0.0
    ).astype(BF16)

    loads["east"].wait()
    loads["north"].wait()

    def edges(e):
        north_rows, south_rows = row_in[e, 0], row_in[e, 1]
        north_rows = jnp.where(oy == n_oy - 1, 0.0, north_rows)
        south_rows = jnp.where(oy == 0, 0.0, south_rows)
        return north_rows, south_rows, col_in[e, 0], col_in[e, 1]

    for copy in halo:
        copy.wait_recv()
    at_east, at_west = lane == COLS - 1, lane == 0
    at_north, at_south = row == ROWS - 1, row == 0

    def sides(x, k, halo_in):
        north_rows, south_rows, west_cols, east_cols = halo_in
        east = jnp.where(at_east, shift(east_cols, COLS - 2 - 2 * k, 1), shift(x, -1, 1))
        west = jnp.where(at_west, shift(west_cols, -2 * k, 1), shift(x, 1, 1))
        north = jnp.where(at_north, north_rows[k : k + 1], shift(x, -1, 0))
        south = jnp.where(at_south, south_rows[k : k + 1], shift(x, 1, 0))
        return east, west, north, south

    halo_in = edges(0)
    wet_east, wet_west, wet_north, wet_south = sides(wet, FIELDS, halo_in)
    coefs = []
    for level in range(LEVELS):
        u, v = east_v[level], north_v[level]
        ce = wet * (LATERAL * wet_east - jnp.minimum(u, 0.0))
        cw = wet * (LATERAL * wet_west + jnp.maximum(u, 0.0))
        cn = wet * (LATERAL * wet_north - jnp.minimum(v, 0.0))
        cs = wet * (LATERAL * wet_south + jnp.maximum(v, 0.0))
        coefs.append((1.0 - (ce + cw + cn + cs), ce, cw, cn, cs))
    mix = VERTICAL * wet

    def lateral(x, level, near):
        c0, ce, cw, cn, cs = coefs[level]
        east, west, north, south = near
        return c0 * x + ce * east + cw * west + cn * north + cs * south

    def slot(level, t):
        return level * TRACERS + t

    upper, lower = [], []
    for t in range(TRACERS):
        x = [first[t * LEVELS + level] for level in range(LEVELS)]
        y = [lateral(x[level], level, sides(x[level], t * LEVELS + level, halo_in)) for level in range(LEVELS)]
        d12, d23 = mix * (x[2] - x[1]), mix * (x[3] - x[2])
        y = [y[0], y[1] + d12, y[2] + d23 - d12, y[3] - d23]
        for level in range(LEVELS):
            state_v[pl.ds(slot(level, t) * ROWS, ROWS), :] = y[level]

    def send_edges(e, level):
        base = level * TRACERS * ROWS
        skip = 0 if level == 0 else -2
        row_out[e, 0, 0:8, :] = state_v[pl.ds(base + skip * ROWS, 8, stride=ROWS), :]
        row_out[e, 1, 0:8, :] = state_v[pl.ds(base + skip * ROWS + ROWS - 1, 8, stride=ROWS), :]
        col_out[e] = pack([state_v[pl.ds(base + k * ROWS, ROWS), :] for k in range(2 * TRACERS)])
        copies = halo_copies(e)
        for copy in copies:
            copy.start()
        return copies

    deep = send_edges(1, 2)

    def placed(groups):
        total = None
        for g in groups:
            got = recv_v[g]
            high = got.astype(BF16)
            rest = (got - high.astype(F32)).astype(BF16)
            lhs = place[:, g * CAP * FLUX : (g + 1) * CAP * FLUX]
            term = jnp.dot(lhs, high, preferred_element_type=F32) + jnp.dot(lhs, rest, preferred_element_type=F32)
            total = term if total is None else total + term
        return total

    for g in NEAR:
        if g != REACH:
            parts[g].wait_recv()
    ocean = placed(NEAR)
    for g in FAR:
        parts[g].wait_recv()
    ocean = ocean + placed(FAR)
    ocean_o[...] = ocean
    q = ocean[(FLUX - 1) * ROWS :]
    top = wet * (0.05 + 0.15 * q * q / (1.0 + q * q))
    surface = [GAIN * wet * ocean[t * ROWS : (t + 1) * ROWS] for t in range(TRACERS)]

    for t in range(TRACERS):
        d01 = top * (first[t * LEVELS + 1] - first[t * LEVELS])
        for level, change in ((0, d01 + surface[t]), (1, -d01)):
            where = pl.ds(slot(level, t) * ROWS, ROWS)
            state_v[where, :] = state_v[where, :] + change
    shallow = send_edges(2, 0)

    for copy in deep:
        copy.wait_recv()
    halo_in = edges(1)
    state = [[state_v[pl.ds(slot(level, t) * ROWS, ROWS), :] for level in range(LEVELS)] for t in range(TRACERS)]
    skip = 2 * TRACERS
    for t in range(TRACERS):
        x = state[t]
        d12, d23 = mix * (x[2] - x[1]), mix * (x[3] - x[2])
        for level, change in ((2, d23 - d12), (3, -d23)):
            k = slot(level, t) - skip
            north_rows, south_rows, west_cols, east_cols = halo_in
            near = sides(x[level], k, (north_rows[2:8], south_rows[2:8], west_cols, east_cols))
            new_o[pl.ds((t * LEVELS + level) * ROWS, ROWS), :] = lateral(x[level], level, near) + change
    for copy in shallow:
        copy.wait_recv()
    halo_in = edges(2)
    for t in range(TRACERS):
        x = state[t]
        d01, d12 = top * (x[1] - x[0]), mix * (x[2] - x[1])
        for level, change in ((0, d01 + surface[t]), (1, d12 - d01)):
            near = sides(x[level], slot(level, t), halo_in)
            new_o[pl.ds((t * LEVELS + level) * ROWS, ROWS), :] = lateral(x[level], level, near) + change

    for g in parts:
        parts[g].wait_send()
    for copy in halo + deep + shallow:
        copy.wait_send()


def body(
    atm_flux, remap_weight, source_block, send_counts, recv_rows, land_mask, tracers, east_velocity, north_velocity
):
    hbm = pl.BlockSpec(memory_space=pltpu.HBM)
    vmem = pl.BlockSpec(memory_space=pltpu.VMEM)
    ocean, new = pl.pallas_call(
        kernel,
        out_shape=(
            jax.ShapeDtypeStruct((FLUX * ROWS, COLS), F32),
            jax.ShapeDtypeStruct((FIELDS * ROWS, COLS), F32),
        ),
        in_specs=[hbm] * 9,
        out_specs=(vmem, vmem),
        scratch_shapes=[
            pltpu.VMEM((FLUX, BLOCKS * COLS), BF16),
            pltpu.VMEM((SLOTS, COLS, COLS), BF16),
            pltpu.VMEM((1, SLOTS), jnp.int32),
            pltpu.VMEM((1, GROUPS), jnp.int32),
            pltpu.VMEM((1, SLOTS), jnp.int32),
            pltpu.VMEM((ROWS, COLS), jnp.int32),
            pltpu.VMEM((FIELDS * ROWS, COLS), F32),
            pltpu.VMEM((LEVELS, ROWS, COLS), F32),
            pltpu.VMEM((LEVELS, ROWS, COLS), F32),
            pltpu.VMEM((FLUX * SLOTS, 2 * COLS), BF16),
            pltpu.VMEM((GROUPS, FLUX * CAP, COLS), F32),
            pltpu.VMEM((GROUPS, FLUX * CAP, COLS), F32),
            pltpu.VMEM((FIELDS * ROWS, COLS), F32),
            pltpu.VMEM((3, ROWS, COLS), F32),
            pltpu.VMEM((3, 2, ROWS, COLS), F32),
            pltpu.VMEM((3, 2, ROWS, COLS), F32),
            pltpu.VMEM((3, 2, ROWS, COLS), F32),
            pltpu.SemaphoreType.DMA((8,)),
            pltpu.SemaphoreType.DMA((GROUPS,)),
            pltpu.SemaphoreType.DMA((GROUPS,)),
            pltpu.SemaphoreType.DMA((GROUPS,)),
            pltpu.SemaphoreType.DMA((3, 4)),
            pltpu.SemaphoreType.DMA((3, 4)),
        ],
        compiler_params=pltpu.CompilerParams(
            collective_id=0, has_side_effects=True, vmem_limit_bytes=32 * 1024 * 1024
        ),
    )(*(pltpu.with_memory_space_constraint(a, pltpu.HBM) for a in (
        atm_flux.reshape(FLUX, BLOCKS * COLS),
        remap_weight.reshape(SLOTS, COLS, COLS),
        source_block,
        send_counts,
        recv_rows,
        land_mask,
        tracers.reshape(FIELDS * ROWS, COLS),
        east_velocity,
        north_velocity,
    )))
    return (ocean.reshape(FLUX, ROWS, COLS), new.reshape(TRACERS, LEVELS, ROWS, COLS))


def solution(mesh):
    in_specs = (
        P(None, "oy", "ox"),
        P("oy", "ox", None, None),
        P("oy", "ox"),
        P("oy", "ox"),
        P("oy", "ox"),
        P("oy", "ox"),
        P(None, None, "oy", "ox"),
        P(None, "oy", "ox"),
        P(None, "oy", "ox"),
    )
    out_specs = (P(None, "oy", "ox"), P(None, None, "oy", "ox"))
    return jax.shard_map(body, mesh=mesh, in_specs=in_specs, out_specs=out_specs, check_vma=False)
```

```python
import jax
import jax.numpy as jnp
from jax import lax
from jax.experimental import pallas as pl
from jax.experimental.pallas import tpu as pltpu
from jax.sharding import PartitionSpec as P

MESH = pl.DeviceIdType.MESH
FLUX = 4
TRACERS = 3
LEVELS = 4
FIELDS = TRACERS * LEVELS
ROWS = 16
COLS = 128
BLOCKS = 6
REACH = 3
CAP = 8
GROUPS = 7
SLOTS = GROUPS * CAP
RING = 8
SPAN = REACH + 1
OFFSETS = (-4, -3, -2, -1, 1, 2, 3, 4)
SENDS = (1, 2, 3, 4, -4, -3, -2, -1)
DATA = 32
AHEAD = (6, 5, 4, 3)
BEHIND = (0, 1, 2)
EAST_AT = 16
NORTH_AT = 20
LATERAL = 0.08
VERTICAL = 0.1
GAIN = 0.5
F32 = jnp.float32
BF16 = jnp.bfloat16


def lanes(shape):
    return lax.broadcasted_iota(jnp.int32, shape, len(shape) - 1)


def rows(shape):
    return lax.broadcasted_iota(jnp.int32, shape, len(shape) - 2)


def kernel(
    flux_h, weight_h, source_h, count_h, recv_h, land_h, tracer_h, east_h, north_h,
    ocean_o, new_o,
    flux_v, weight_v, source_v, count_v, place_v, land_v, tracer_v, east_v, north_v,
    lhs_v, part_v, edge_v, send_v, recv_v, state_v, col_out, col_in, row_out, row_in,
    load_sem, weight_sem, part_send, part_recv, halo_send, halo_recv, ack_sem,
):
    oy, ox = lax.axis_index("oy"), lax.axis_index("ox")
    n_oy, n_ox = lax.axis_size("oy"), lax.axis_size("ox")

    def along(offset):
        return (oy, lax.rem(ox + (n_ox + offset), n_ox))

    up = (lax.rem(oy + 1, n_oy), ox)
    down = (lax.rem(oy + (n_oy - 1), n_oy), ox)

    loads = {}
    for i, (name, src, dst) in enumerate((
        ("tracer", tracer_h, tracer_v), ("land", land_h, land_v), ("flux", flux_h, flux_v),
        ("source", source_h, source_v), ("count", count_h, count_v), ("place", recv_h, place_v),
        ("east", east_h, east_v), ("north", north_h, north_v),
    )):
        loads[name] = pltpu.make_async_copy(src, dst, load_sem.at[i])
    weights = {
        g: pltpu.make_async_copy(
            weight_h.at[pl.ds(g * CAP, CAP)], weight_v.at[pl.ds(g * CAP, CAP)], weight_sem.at[g]
        )
        for g in range(GROUPS)
    }
    for name in ("flux", "source", "count", "tracer", "land", "place", "east", "north"):
        loads[name].start()
    for g in AHEAD + BEHIND:
        weights[g].start()

    key = lax.rem(ox, RING)
    odd = lax.rem(oy, 2)
    partners = {d: along(d) for d in OFFSETS}
    partners["up"], partners["down"] = up, down
    later = {d: lax.rem(key + (d + RING), RING) > key for d in OFFSETS}
    later["up"] = (odd == 1) & (oy != n_oy - 1)
    later["down"] = (odd == 1) | (oy == 0)
    opposite = {d: -d for d in OFFSETS} | {"up": "down", "down": "up"}
    place_of = {d: i for i, d in enumerate(partners)}
    barrier = pltpu.get_barrier_semaphore()
    announced = jnp.int32(0)
    for d in partners:
        announced += jnp.where(later[d], 0, 1)

        @pl.when(later[d])
        def _():
            pl.semaphore_signal(barrier, inc=1, device_id=partners[d], device_id_type=MESH)

    def remote(src, dst, send, recv, device):
        return pltpu.make_async_remote_copy(
            src_ref=src, dst_ref=dst, send_sem=send, recv_sem=recv, device_id=device, device_id_type=MESH
        )

    def row_copies(e):
        return {
            "down": remote(row_out.at[e, 0], row_in.at[e, 0], halo_send.at[e, 0], halo_recv.at[e, 0], down),
            "up": remote(row_out.at[e, 1], row_in.at[e, 1], halo_send.at[e, 1], halo_recv.at[e, 1], up),
        }

    first_rows = row_copies(0)
    columns = {
        1: remote(col_out.at[0], col_in.at[0], halo_send.at[2, 0], halo_recv.at[2, 0], partners[1]),
        -1: remote(col_out.at[1], col_in.at[1], halo_send.at[2, 1], halo_recv.at[2, 1], partners[-1]),
    }
    parts = {}
    for d in OFFSETS:
        if abs(d) <= REACH:
            src, dst = send_v.at[d + REACH], recv_v.at[d + SPAN]
        else:
            src, dst = edge_v.at[int(d > 0)], recv_v.at[d + SPAN, pl.ds(DATA, 8)]
        parts[d] = remote(src, dst, part_send.at[d + SPAN], part_recv.at[d + SPAN], partners[d])

    lane = lanes((ROWS, COLS))
    row = rows((ROWS, COLS))

    def shift(x, by, axis):
        return pltpu.roll(x, by % x.shape[axis], axis)

    for name in ("flux", "source", "count", "tracer", "land", "place", "east", "north"):
        loads[name].wait()
    flux = flux_v[...].astype(F32)
    blocks = jnp.concatenate([flux[:, n * COLS : (n + 1) * COLS] for n in range(BLOCKS)], axis=0)
    blocks = jnp.concatenate([blocks, jnp.zeros((COLS - FLUX * BLOCKS, COLS), F32)], axis=0).astype(BF16)
    wide = FLUX * SLOTS
    at_slot = rows((wide, SLOTS)) // FLUX == lanes((wide, SLOTS))
    at_group = rows((wide, GROUPS)) // DATA == lanes((wide, GROUPS))
    source = jnp.where(at_slot, source_v[...].astype(F32), 0.0).astype(BF16)
    count = jnp.where(at_group, count_v[...].astype(F32), 0.0).astype(BF16)
    source = jnp.dot(source, jnp.ones((SLOTS, COLS), BF16), preferred_element_type=F32)
    count = jnp.dot(count, jnp.ones((GROUPS, COLS), BF16), preferred_element_type=F32)
    r, c = rows((wide, COLS)), lanes((wide, COLS))
    pick = (
        (source == (c // FLUX).astype(F32))
        & (r % FLUX == c % FLUX)
        & (((r // FLUX) % CAP).astype(F32) < count)
    )
    chosen = jnp.dot(jnp.where(pick, 1.0, 0.0).astype(BF16), blocks, preferred_element_type=F32)
    low = r % 16 < 8
    lhs_v[:, 0:COLS] = jnp.where(low, chosen, 0.0).astype(BF16)
    lhs_v[:, COLS : 2 * COLS] = jnp.where(low, 0.0, chosen).astype(BF16)

    wet = land_v[...].astype(F32)
    first = [tracer_v[pl.ds(k * ROWS, ROWS), :] for k in range(FIELDS)]
    for side, at in ((0, 0), (1, ROWS - 1)):
        row_out[0, side, 0:FIELDS, :] = tracer_v[pl.ds(at, FIELDS, stride=ROWS), :]
        row_out[0, side, FIELDS:ROWS, :] = jnp.broadcast_to(wet[at : at + 1], (ROWS - FIELDS, COLS))
    packed = {k: first[k] for k in range(FIELDS)} | {FIELDS: wet}
    packed |= {EAST_AT + k: east_v[k] for k in range(LEVELS)} | {NORTH_AT + k: north_v[k] for k in range(LEVELS)}
    to_east = jnp.zeros((ROWS, COLS), F32)
    to_west = jnp.zeros((ROWS, COLS), F32)
    for k, field in packed.items():
        to_east = jnp.where(lane // 2 == k, shift(field, 2 * k + 2, 1), to_east)
        to_west = jnp.where(lane // 2 == k, shift(field, 2 * k, 1), to_west)
    margin = jnp.broadcast_to(place_v[...].astype(F32), (8, SLOTS)).astype(BF16)
    same = jnp.where(lanes((SLOTS, COLS)) == rows((SLOTS, COLS)), 1.0, 0.0).astype(BF16)
    margin = jnp.dot(margin, same, preferred_element_type=F32)
    for i, value in enumerate((to_east, to_west)):
        col_out[i, 0:ROWS, :] = value
        col_out[i, ROWS:, :] = margin

    half = rows((16, COLS)) % 8 < 4
    edge_row = rows((8, COLS))
    ends = jnp.where(lanes((8, COLS)) == jnp.where(edge_row < 2, 0, COLS - 1), 1.0, 0.0).astype(BF16)
    dims = (((1,), (1,)), ((), ()))

    def split(x):
        high = x.astype(BF16)
        return high, (x - high.astype(F32)).astype(BF16)

    def remap(groups):
        for g in groups:
            weights[g].wait()
        for g in groups:
            for q in (2 * g, 2 * g + 1):
                w = [weight_v[4 * q + j] for j in range(4)]
                tile = jnp.concatenate(
                    [jnp.concatenate(w[0:2], axis=1), jnp.concatenate(w[2:4], axis=1)], axis=0
                )
                both = jnp.dot(lhs_v[pl.ds(16 * q, 16), :], tile, preferred_element_type=F32)
                value = jnp.where(half, both[:, 0:COLS], both[:, COLS:])
                part_v[pl.ds(16 * q, 16), :] = value
                if g == REACH:
                    recv_v[SPAN, pl.ds(16 * (q - 2 * g), 16), :] = value
                else:
                    send_v[g, pl.ds(16 * (q - 2 * g), 16), :] = value

    def edge_columns(base, groups, at):
        high, rest = split(part_v[pl.ds(base * DATA, COLS), :])
        edge = lax.dot_general(ends, high, dims, preferred_element_type=F32)
        edge = edge + lax.dot_general(ends, rest, dims, preferred_element_type=F32)
        for g in groups:
            send_v[g, DATA:, :] = edge
        edge_v[at] = edge

    remap(AHEAD)
    edge_columns(REACH, AHEAD[:-1], 1)

    @pl.when(announced > 0)
    def _():
        pl.semaphore_wait(barrier, announced)

    for d in partners:
        @pl.when(jnp.logical_not(later[d]))
        def _():
            pl.semaphore_signal(
                ack_sem.at[place_of[opposite[d]]], inc=1, device_id=partners[d], device_id_type=MESH
            )

    @pl.when(jnp.logical_not(later[1]))
    def _():
        columns[1].start()
    for d in SENDS[0:SPAN]:
        @pl.when(jnp.logical_not(later[d]))
        def _():
            parts[d].start()

    remap(BEHIND)
    edge_columns(0, BEHIND, 0)

    for d in SENDS[SPAN:]:
        @pl.when(jnp.logical_not(later[d]))
        def _():
            parts[d].start()
    for d, copy in (("up", first_rows["up"]), ("down", first_rows["down"]), (-1, columns[-1])):
        @pl.when(jnp.logical_not(later[d]))
        def _():
            copy.start()
    for d in ("up", "down"):
        @pl.when(later[d])
        def _():
            pl.semaphore_wait(ack_sem.at[place_of[d]], 1)
            first_rows[d].start()
    for d in SENDS:
        @pl.when(later[d])
        def _():
            pl.semaphore_wait(ack_sem.at[place_of[d]], 1)
            if d in columns:
                columns[d].start()
            parts[d].start()

    def edges(e):
        north_rows, south_rows = row_in[e, 0], row_in[e, 1]
        north_rows = jnp.where(oy == n_oy - 1, 0.0, north_rows)
        south_rows = jnp.where(oy == 0, 0.0, south_rows)
        return north_rows, south_rows

    for copy in (*first_rows.values(), *columns.values()):
        copy.wait_recv()
    at_east, at_west = lane == COLS - 1, lane == 0
    at_north, at_south = row == ROWS - 1, row == 0
    north_rows, south_rows = edges(0)
    from_west, from_east = col_in[0, 0:ROWS], col_in[1, 0:ROWS]

    def to_edge(x, k, side):
        return shift(x, COLS - 1 - 2 * k, 1) if side == "east" else shift(x, -2 * k - 1, 1)

    def sides(x, k):
        east = jnp.where(at_east, to_edge(from_east, k, "east"), shift(x, -1, 1))
        west = jnp.where(at_west, to_edge(from_west, k, "west"), shift(x, 1, 1))
        north = jnp.where(at_north, north_rows[k : k + 1], shift(x, -1, 0))
        south = jnp.where(at_south, south_rows[k : k + 1], shift(x, 1, 0))
        return east, west, north, south

    wet_east, wet_west, wet_north, wet_south = sides(wet, FIELDS)
    coefs = []
    for level in range(LEVELS):
        u, v = east_v[level], north_v[level]
        ce = wet * (LATERAL * wet_east - jnp.minimum(u, 0.0))
        cw = wet * (LATERAL * wet_west + jnp.maximum(u, 0.0))
        cn = wet * (LATERAL * wet_north - jnp.minimum(v, 0.0))
        cs = wet * (LATERAL * wet_south + jnp.maximum(v, 0.0))
        coefs.append((1.0 - (ce + cw + cn + cs), ce, cw, cn, cs))
    mix = VERTICAL * wet

    def lateral(x, level, near):
        c0, ce, cw, cn, cs = coefs[level]
        east, west, north, south = near
        return c0 * x + ce * east + cw * west + cn * north + cs * south

    for t in range(TRACERS):
        x = first[t * LEVELS : (t + 1) * LEVELS]
        y = [lateral(x[level], level, sides(x[level], t * LEVELS + level)) for level in range(LEVELS)]
        d12, d23 = mix * (x[2] - x[1]), mix * (x[3] - x[2])
        for level, value in enumerate((y[0], y[1] + d12, y[2] + d23 - d12, y[3] - d23)):
            state_v[pl.ds((t * LEVELS + level) * ROWS, ROWS), :] = value

    lists = jnp.where(edge_row == 0, margin, jnp.where(edge_row == 1, col_in[0, ROWS:], col_in[1, ROWS:]))
    c = lanes((COLS, 2 * COLS))
    slot_at = jnp.where(c < COLS, c // FLUX, (c - COLS) // FLUX + REACH * CAP)
    expand = jnp.where(slot_at == rows((COLS, 2 * COLS)), 1.0, 0.0).astype(BF16)
    target_row = jnp.dot(lists.astype(BF16), expand, preferred_element_type=F32)
    r, c = rows((FLUX * ROWS, 2 * COLS)), lanes((FLUX * ROWS, 2 * COLS))
    place = jnp.where(
        (target_row[0:1] == (r % ROWS).astype(F32)) & (c % FLUX == r // ROWS), 1.0, 0.0
    ).astype(BF16)
    r = rows((ROWS, 2 * COLS)).astype(F32)
    on_row = [target_row[i : i + 1] == r for i in (1, 2)]
    c = lanes((2 * COLS, 2 * COLS))
    gather = jnp.where(
        rows((2 * COLS, 2 * COLS)) % FLUX == jnp.where(c < COLS, FLUX - 1, (c - COLS) // (2 * LEVELS)), 1.0, 0.0
    ).astype(BF16)

    level_of = (lane // 2) % LEVELS

    def beside(i):
        if i == 0:
            x, own, way, own_wet = from_west, to_west, 1, to_west[:, 2 * FIELDS : 2 * FIELDS + 1]
        else:
            x, own, way, own_wet = from_east, to_east, -1, to_east[:, 2 * FIELDS + 1 : 2 * FIELDS + 2]
        center = 2 * FIELDS + (1 - i)
        wet_c = jnp.broadcast_to(x[:, center : center + 1], (ROWS, COLS))
        wet_far = jnp.broadcast_to(x[:, center - way : center - way + 1], (ROWS, COLS))
        wet_own = jnp.broadcast_to(own_wet, (ROWS, COLS))

        def spread(at):
            moved = [shift(x, 2 * (t * LEVELS - at), 1) for t in range(TRACERS)]
            return jnp.where(lane < 2 * LEVELS, moved[0], jnp.where(lane < 4 * LEVELS, moved[1], moved[2]))

        u, v = spread(EAST_AT), spread(NORTH_AT)
        far, own = shift(x, way, 1), shift(own, way, 1)
        plus, minus = jnp.maximum(u, 0.0), -jnp.minimum(u, 0.0)
        c_far, c_own = (plus, minus) if i == 0 else (minus, plus)
        change = (LATERAL * wet_far + c_far) * (far - x) + (LATERAL * wet_own + c_own) * (own - x)
        step = shift(x, -2, 1) - x
        return x, wet_c, v, change, step

    halves = [beside(0), beside(1)]

    for d in OFFSETS:
        parts[d].wait_recv()
    arrived = [recv_v[g - REACH + SPAN, 0:DATA] for g in range(GROUPS)]
    arrived = jnp.concatenate(arrived[:SPAN] + [jnp.zeros((DATA, COLS), F32)] + arrived[SPAN:], axis=0)
    high, rest = split(arrived)
    ocean = jnp.dot(place, high, preferred_element_type=F32) + jnp.dot(place, rest, preferred_element_type=F32)
    ocean_o[...] = ocean
    q = ocean[(FLUX - 1) * ROWS :]
    top = wet * (0.05 + 0.15 * q * q / (1.0 + q * q))
    surface = [GAIN * wet * ocean[t * ROWS : (t + 1) * ROWS] for t in range(TRACERS)]
    for t in range(TRACERS):
        d01 = top * (first[t * LEVELS + 1] - first[t * LEVELS])
        for level, change in ((0, d01 + surface[t]), (1, -d01)):
            where = pl.ds((t * LEVELS + level) * ROWS, ROWS)
            state_v[where, :] = state_v[where, :] + change

    for side, at in ((0, 0), (1, ROWS - 1)):
        row_out[1, side, 0:FIELDS, :] = state_v[pl.ds(at, FIELDS, stride=ROWS), :]
        row_out[1, side, FIELDS : FIELDS + 1, :] = from_west[at : at + 1]
        row_out[1, side, FIELDS + 1 : FIELDS + 2, :] = from_east[at : at + 1]
        row_out[1, side, FIELDS + 2 :, :] = jnp.zeros((2, COLS), F32)
    second_rows = row_copies(1)
    for copy in second_rows.values():
        copy.start()

    quarter = lanes((8, COLS)) // DATA

    def along_lanes(base, at):
        out = [jnp.zeros((8, COLS), F32)] * 2
        for g in range(GROUPS):
            d = base + g
            ahead = d > 0 or (d == 0 and base != -2)
            value = recv_v[d + SPAN, DATA:] if d != 0 else edge_v[int(ahead)]
            out[ahead] = jnp.where(quarter == (g - REACH if ahead else g), value, out[ahead])
        return jnp.concatenate([tile[at : at + 1] for tile in out], axis=1)

    terms = [
        jnp.where(on_row[0], along_lanes(-2, 2), 0.0),
        jnp.where(on_row[1], along_lanes(-4, 0), 0.0),
    ]
    high, rest = split(jnp.concatenate(terms, axis=0))
    margins = jnp.dot(high, gather, preferred_element_type=F32) + jnp.dot(rest, gather, preferred_element_type=F32)
    inner = []
    for i, (x, wet_c, v, change, step) in enumerate(halves):
        q = margins[i * ROWS : (i + 1) * ROWS, 0:COLS]
        kv = 0.05 + 0.15 * q * q / (1.0 + q * q)
        face = jnp.where(level_of == LEVELS - 1, 0.0, jnp.where(level_of == 0, kv, VERTICAL) * step)
        source = jnp.where(level_of == 0, GAIN * margins[i * ROWS : (i + 1) * ROWS, COLS:], shift(-face, 2, 1))
        inner.append(change + face + source)

    for t in range(TRACERS):
        x = [state_v[pl.ds((t * LEVELS + level) * ROWS, ROWS), :] for level in range(LEVELS)]
        d01, d12, d23 = top * (x[1] - x[0]), mix * (x[2] - x[1]), mix * (x[3] - x[2])
        changes = (d01 + surface[t], d12 - d01, d23 - d12, -d23)
        for level, change in enumerate(changes):
            y = x[level]
            near = (
                jnp.where(at_east, 0.0, shift(y, -1, 1)),
                jnp.where(at_west, 0.0, shift(y, 1, 1)),
                jnp.where(at_north, 0.0, shift(y, -1, 0)),
                jnp.where(at_south, 0.0, shift(y, 1, 0)),
            )
            new_o[pl.ds((t * LEVELS + level) * ROWS, ROWS), :] = lateral(y, level, near) + change

    for copy in second_rows.values():
        copy.wait_recv()
    north_rows, south_rows = edges(1)
    halo = []
    for i, ((x, wet_c, v, _, _), change) in enumerate(zip(halves, inner)):
        north = jnp.where(at_north, north_rows[FIELDS + i : FIELDS + i + 1], shift(x, -1, 0))
        south = jnp.where(at_south, south_rows[FIELDS + i : FIELDS + i + 1], shift(x, 1, 0))
        center = 2 * FIELDS + (1 - i)
        wet_n = jnp.broadcast_to(north[:, center : center + 1], (ROWS, COLS))
        wet_s = jnp.broadcast_to(south[:, center : center + 1], (ROWS, COLS))
        change = change + (LATERAL * wet_n - jnp.minimum(v, 0.0)) * (north - x)
        change = change + (LATERAL * wet_s + jnp.maximum(v, 0.0)) * (south - x)
        halo.append(x + wet_c * change)
    for level in range(LEVELS):
        _, ce, cw, cn, cs = coefs[level]
        ce, cw = jnp.where(at_east, ce, 0.0), jnp.where(at_west, cw, 0.0)
        cn, cs = jnp.where(at_north, cn, 0.0), jnp.where(at_south, cs, 0.0)
        for t in range(TRACERS):
            k = t * LEVELS + level
            where = pl.ds(k * ROWS, ROWS)
            new_o[where, :] = (
                new_o[where, :]
                + cw * to_edge(halo[0], k, "west")
                + ce * to_edge(halo[1], k, "east")
                + cn * north_rows[k : k + 1]
                + cs * south_rows[k : k + 1]
            )

    for copy in (*parts.values(), *first_rows.values(), *columns.values(), *second_rows.values()):
        copy.wait_send()


def store(ocean_v, new_v, ocean_o, new_o, sem):
    copies = [
        pltpu.make_async_copy(new_v, new_o, sem.at[0]),
        pltpu.make_async_copy(ocean_v, ocean_o, sem.at[1]),
    ]
    for copy in copies:
        copy.start()
    for copy in copies:
        copy.wait()


def body(
    atm_flux, remap_weight, source_block, send_counts, recv_rows, land_mask, tracers, east_velocity, north_velocity
):
    hbm = pl.BlockSpec(memory_space=pltpu.HBM)
    vmem = pl.BlockSpec(memory_space=pltpu.VMEM)
    ocean, new = pl.pallas_call(
        kernel,
        out_shape=(
            jax.ShapeDtypeStruct((FLUX * ROWS, COLS), F32),
            jax.ShapeDtypeStruct((FIELDS * ROWS, COLS), F32),
        ),
        in_specs=[hbm] * 9,
        out_specs=(vmem, vmem),
        scratch_shapes=[
            pltpu.VMEM((FLUX, BLOCKS * COLS), BF16),
            pltpu.VMEM((SLOTS, COLS, COLS), BF16),
            pltpu.VMEM((1, SLOTS), jnp.int32),
            pltpu.VMEM((1, GROUPS), jnp.int32),
            pltpu.VMEM((1, SLOTS), jnp.int32),
            pltpu.VMEM((ROWS, COLS), jnp.int32),
            pltpu.VMEM((FIELDS * ROWS, COLS), F32),
            pltpu.VMEM((LEVELS, ROWS, COLS), F32),
            pltpu.VMEM((LEVELS, ROWS, COLS), F32),
            pltpu.VMEM((FLUX * SLOTS, 2 * COLS), BF16),
            pltpu.VMEM((FLUX * SLOTS, COLS), F32),
            pltpu.VMEM((2, 8, COLS), F32),
            pltpu.VMEM((GROUPS, DATA + 8, COLS), F32),
            pltpu.VMEM((2 * SPAN + 1, DATA + 8, COLS), F32),
            pltpu.VMEM((FIELDS * ROWS, COLS), F32),
            pltpu.VMEM((2, ROWS + 8, COLS), F32),
            pltpu.VMEM((2, ROWS + 8, COLS), F32),
            pltpu.VMEM((2, 2, ROWS, COLS), F32),
            pltpu.VMEM((2, 2, ROWS, COLS), F32),
            pltpu.SemaphoreType.DMA((8,)),
            pltpu.SemaphoreType.DMA((GROUPS,)),
            pltpu.SemaphoreType.DMA((2 * SPAN + 1,)),
            pltpu.SemaphoreType.DMA((2 * SPAN + 1,)),
            pltpu.SemaphoreType.DMA((3, 2)),
            pltpu.SemaphoreType.DMA((3, 2)),
            pltpu.SemaphoreType.REGULAR((len(OFFSETS) + 2,)),
        ],
        compiler_params=pltpu.CompilerParams(
            collective_id=0, has_side_effects=True, vmem_limit_bytes=32 * 1024 * 1024
        ),
    )(*(pltpu.with_memory_space_constraint(a, pltpu.HBM) for a in (
        atm_flux.reshape(FLUX, BLOCKS * COLS),
        remap_weight.reshape(SLOTS, COLS, COLS),
        source_block,
        send_counts,
        recv_rows,
        land_mask,
        tracers.reshape(FIELDS * ROWS, COLS),
        east_velocity,
        north_velocity,
    )))
    ocean, new = pl.pallas_call(
        store,
        out_shape=(
            jax.ShapeDtypeStruct((FLUX * ROWS, COLS), F32),
            jax.ShapeDtypeStruct((FIELDS * ROWS, COLS), F32),
        ),
        in_specs=[vmem, vmem],
        out_specs=(hbm, hbm),
        scratch_shapes=[pltpu.SemaphoreType.DMA((2,))],
    )(*(pltpu.with_memory_space_constraint(a, pltpu.VMEM) for a in (ocean, new)))
    return (ocean.reshape(FLUX, ROWS, COLS), new.reshape(TRACERS, LEVELS, ROWS, COLS))


def solution(mesh):
    in_specs = (
        P(None, "oy", "ox"),
        P("oy", "ox", None, None),
        P("oy", "ox"),
        P("oy", "ox"),
        P("oy", "ox"),
        P("oy", "ox"),
        P(None, None, "oy", "ox"),
        P(None, "oy", "ox"),
        P(None, "oy", "ox"),
    )
    out_specs = (P(None, "oy", "ox"), P(None, None, "oy", "ox"))
    return jax.shard_map(body, mesh=mesh, in_specs=in_specs, out_specs=out_specs, check_vma=False)
```

```python
import jax
import jax.numpy as jnp
from jax import lax
from jax.experimental import pallas as pl
from jax.experimental.pallas import tpu as pltpu
from jax.sharding import PartitionSpec as P

MESH = pl.DeviceIdType.MESH
FLUX = 4
TRACERS = 3
LEVELS = 4
FIELDS = TRACERS * LEVELS
ROWS = 16
COLS = 128
BLOCKS = 6
REACH = 3
CAP = 8
GROUPS = 7
SLOTS = GROUPS * CAP
RING = 8
SPAN = REACH + 1
OFFSETS = (-4, -3, -2, -1, 1, 2, 3, 4)
SENDS = (1, 2, 3, 4, -4, -3, -2, -1)
DATA = 32
AHEAD = (6, 5, 4, 3)
BEHIND = (0, 1, 2)
EAST_AT = 16
NORTH_AT = 20
LATERAL = 0.08
VERTICAL = 0.1
GAIN = 0.5
F32 = jnp.float32
BF16 = jnp.bfloat16


def lanes(shape):
    return lax.broadcasted_iota(jnp.int32, shape, len(shape) - 1)


def rows(shape):
    return lax.broadcasted_iota(jnp.int32, shape, len(shape) - 2)


def kernel(
    flux_h, weight_h, source_h, count_h, recv_h, land_h, tracer_h, east_h, north_h,
    ocean_o, new_o,
    flux_v, weight_v, source_v, count_v, place_v, land_v, tracer_v, east_v, north_v,
    lhs_v, part_v, edge_v, send_v, recv_v, state_v, col_out, col_in, row_out, row_in,
    load_sem, weight_sem, part_send, part_recv, halo_send, halo_recv, ack_sem,
):
    oy, ox = lax.axis_index("oy"), lax.axis_index("ox")
    n_oy, n_ox = lax.axis_size("oy"), lax.axis_size("ox")

    def along(offset):
        return (oy, lax.rem(ox + (n_ox + offset), n_ox))

    up = (lax.rem(oy + 1, n_oy), ox)
    down = (lax.rem(oy + (n_oy - 1), n_oy), ox)

    loads = {}
    for i, (name, src, dst) in enumerate((
        ("tracer", tracer_h, tracer_v), ("land", land_h, land_v), ("flux", flux_h, flux_v),
        ("source", source_h, source_v), ("count", count_h, count_v), ("place", recv_h, place_v),
        ("east", east_h, east_v), ("north", north_h, north_v),
    )):
        loads[name] = pltpu.make_async_copy(src, dst, load_sem.at[i])
    weights = {}
    for i, groups in enumerate((AHEAD, BEHIND)):
        span = pl.ds(min(groups) * CAP, len(groups) * CAP)
        weights[groups] = pltpu.make_async_copy(weight_h.at[span], weight_v.at[span], weight_sem.at[i])
    for name in ("flux", "source", "count", "tracer", "land", "place", "east", "north"):
        loads[name].start()
    for copy in weights.values():
        copy.start()

    key = lax.rem(ox, RING)
    odd = lax.rem(oy, 2)
    partners = {"up": up, "down": down} | {d: along(d) for d in OFFSETS}
    later = {d: lax.rem(key + (d + RING), RING) > key for d in OFFSETS}
    later["up"] = later["down"] = odd == 1
    there = {"up": oy != n_oy - 1, "down": oy != 0}
    late = {d: later[d] & there[d] if d in there else later[d] for d in partners}
    early = {d: jnp.logical_not(later[d]) & there[d] if d in there else jnp.logical_not(later[d]) for d in partners}
    opposite = {d: -d for d in OFFSETS} | {"up": "down", "down": "up"}
    place_of = {d: i for i, d in enumerate(partners)}
    barrier = pltpu.get_barrier_semaphore()
    announced = jnp.int32(0)
    for d in partners:
        announced += jnp.where(early[d], 1, 0)

        @pl.when(late[d])
        def _():
            pl.semaphore_signal(barrier, inc=1, device_id=partners[d], device_id_type=MESH)

    def remote(src, dst, send, recv, device):
        return pltpu.make_async_remote_copy(
            src_ref=src, dst_ref=dst, send_sem=send, recv_sem=recv, device_id=device, device_id_type=MESH
        )

    def row_copies(e):
        return {
            "down": remote(row_out.at[e, 0], row_in.at[e, 0], halo_send.at[e, 0], halo_recv.at[e, 0], down),
            "up": remote(row_out.at[e, 1], row_in.at[e, 1], halo_send.at[e, 1], halo_recv.at[e, 1], up),
        }

    first_rows = row_copies(0)
    columns = {
        1: remote(col_out.at[0], col_in.at[0], halo_send.at[2, 0], halo_recv.at[2, 0], partners[1]),
        -1: remote(col_out.at[1], col_in.at[1], halo_send.at[2, 1], halo_recv.at[2, 1], partners[-1]),
    }
    parts = {}
    for d in OFFSETS:
        if abs(d) <= REACH:
            src, dst = send_v.at[d + REACH], recv_v.at[d + SPAN]
        else:
            src, dst = edge_v.at[int(d > 0)], recv_v.at[d + SPAN, pl.ds(DATA, 8)]
        parts[d] = remote(src, dst, part_send.at[d + SPAN], part_recv.at[d + SPAN], partners[d])

    lane = lanes((ROWS, COLS))
    row = rows((ROWS, COLS))

    def shift(x, by, axis):
        return pltpu.roll(x, by % x.shape[axis], axis)

    for name in ("flux", "source", "count", "tracer", "land", "place", "east", "north"):
        loads[name].wait()
    flux = flux_v[...].astype(F32)
    blocks = jnp.concatenate([flux[:, n * COLS : (n + 1) * COLS] for n in range(BLOCKS)], axis=0)
    blocks = jnp.concatenate([blocks, jnp.zeros((COLS - FLUX * BLOCKS, COLS), F32)], axis=0).astype(BF16)
    wide = FLUX * SLOTS
    at_slot = rows((wide, SLOTS)) // FLUX == lanes((wide, SLOTS))
    at_group = rows((wide, GROUPS)) // DATA == lanes((wide, GROUPS))
    source = jnp.where(at_slot, source_v[...].astype(F32), 0.0).astype(BF16)
    count = jnp.where(at_group, count_v[...].astype(F32), 0.0).astype(BF16)
    source = jnp.dot(source, jnp.ones((SLOTS, COLS), BF16), preferred_element_type=F32)
    count = jnp.dot(count, jnp.ones((GROUPS, COLS), BF16), preferred_element_type=F32)
    r, c = rows((wide, COLS)), lanes((wide, COLS))
    pick = (
        (source == (c // FLUX).astype(F32))
        & (r % FLUX == c % FLUX)
        & (((r // FLUX) % CAP).astype(F32) < count)
    )
    chosen = jnp.dot(jnp.where(pick, 1.0, 0.0).astype(BF16), blocks, preferred_element_type=F32)
    low = r % 16 < 8
    lhs_v[:, 0:COLS] = jnp.where(low, chosen, 0.0).astype(BF16)
    lhs_v[:, COLS : 2 * COLS] = jnp.where(low, 0.0, chosen).astype(BF16)

    wet = land_v[...].astype(F32)
    first = [tracer_v[pl.ds(k * ROWS, ROWS), :] for k in range(FIELDS)]
    for side, at in ((0, 0), (1, ROWS - 1)):
        row_out[0, side, 0:FIELDS, :] = tracer_v[pl.ds(at, FIELDS, stride=ROWS), :]
        row_out[0, side, FIELDS:ROWS, :] = jnp.broadcast_to(wet[at : at + 1], (ROWS - FIELDS, COLS))
    packed = {k: first[k] for k in range(FIELDS)} | {FIELDS: wet}
    packed |= {EAST_AT + k: east_v[k] for k in range(LEVELS)} | {NORTH_AT + k: north_v[k] for k in range(LEVELS)}
    to_east = jnp.zeros((ROWS, COLS), F32)
    to_west = jnp.zeros((ROWS, COLS), F32)
    for k, field in packed.items():
        to_east = jnp.where(lane // 2 == k, shift(field, 2 * k + 2, 1), to_east)
        to_west = jnp.where(lane // 2 == k, shift(field, 2 * k, 1), to_west)
    margin = jnp.broadcast_to(place_v[...].astype(F32), (8, SLOTS)).astype(BF16)
    same = jnp.where(lanes((SLOTS, COLS)) == rows((SLOTS, COLS)), 1.0, 0.0).astype(BF16)
    margin = jnp.dot(margin, same, preferred_element_type=F32)
    for i, value in enumerate((to_east, to_west)):
        col_out[i, 0:ROWS, :] = value
        col_out[i, ROWS:, :] = margin

    half = rows((16, COLS)) % 8 < 4
    edge_row = rows((8, COLS))
    ends = jnp.where(lanes((8, COLS)) == jnp.where(edge_row < 2, 0, COLS - 1), 1.0, 0.0).astype(BF16)
    dims = (((1,), (1,)), ((), ()))

    def split(x):
        high = x.astype(BF16)
        return high, (x - high.astype(F32)).astype(BF16)

    def remap(groups):
        weights[groups].wait()
        for g in groups:
            for q in (2 * g, 2 * g + 1):
                w = [weight_v[4 * q + j] for j in range(4)]
                tile = jnp.concatenate(
                    [jnp.concatenate(w[0:2], axis=1), jnp.concatenate(w[2:4], axis=1)], axis=0
                )
                both = jnp.dot(lhs_v[pl.ds(16 * q, 16), :], tile, preferred_element_type=F32)
                value = jnp.where(half, both[:, 0:COLS], both[:, COLS:])
                part_v[pl.ds(16 * q, 16), :] = value
                if g == REACH:
                    recv_v[SPAN, pl.ds(16 * (q - 2 * g), 16), :] = value
                else:
                    send_v[g, pl.ds(16 * (q - 2 * g), 16), :] = value

    def edge_columns(base, groups, at):
        high, rest = split(part_v[pl.ds(base * DATA, COLS), :])
        edge = lax.dot_general(ends, high, dims, preferred_element_type=F32)
        edge = edge + lax.dot_general(ends, rest, dims, preferred_element_type=F32)
        for g in groups:
            send_v[g, DATA:, :] = edge
        edge_v[at] = edge

    remap(AHEAD)
    edge_columns(REACH, AHEAD[:-1], 1)

    @pl.when(announced > 0)
    def _():
        pl.semaphore_wait(barrier, announced)

    for d in partners:
        @pl.when(early[d])
        def _():
            pl.semaphore_signal(
                ack_sem.at[place_of[opposite[d]]], inc=1, device_id=partners[d], device_id_type=MESH
            )

    @pl.when(early[1])
    def _():
        columns[1].start()
    for d in SENDS[0:SPAN]:
        @pl.when(early[d])
        def _():
            parts[d].start()

    remap(BEHIND)
    edge_columns(0, BEHIND, 0)

    for d in SENDS[SPAN:]:
        @pl.when(early[d])
        def _():
            parts[d].start()
    for d, copy in (("up", first_rows["up"]), ("down", first_rows["down"]), (-1, columns[-1])):
        @pl.when(early[d])
        def _():
            copy.start()
    for d in ("up", "down"):
        @pl.when(late[d])
        def _():
            pl.semaphore_wait(ack_sem.at[place_of[d]], 1)
            first_rows[d].start()
    def edges(e):
        north_rows, south_rows = row_in[e, 0], row_in[e, 1]
        north_rows = jnp.where(oy == n_oy - 1, 0.0, north_rows)
        south_rows = jnp.where(oy == 0, 0.0, south_rows)
        return north_rows, south_rows

    def of_rows(copies, wait):
        for d, copy in copies.items():
            @pl.when(there[d if wait == "send" else opposite[d]])
            def _():
                copy.wait_send() if wait == "send" else copy.wait_recv()

    of_rows(first_rows, "recv")
    at_east, at_west = lane == COLS - 1, lane == 0
    at_north, at_south = row == ROWS - 1, row == 0
    north_rows, south_rows = edges(0)

    def above(x, k):
        return jnp.where(at_north, north_rows[k : k + 1], shift(x, -1, 0))

    def below(x, k):
        return jnp.where(at_south, south_rows[k : k + 1], shift(x, 1, 0))

    wet_east, wet_west = shift(wet, -1, 1), shift(wet, 1, 1)
    wet_north, wet_south = above(wet, FIELDS), below(wet, FIELDS)
    coefs = []
    for level in range(LEVELS):
        u, v = east_v[level], north_v[level]
        ce = jnp.where(at_east, 0.0, wet * (LATERAL * wet_east - jnp.minimum(u, 0.0)))
        cw = jnp.where(at_west, 0.0, wet * (LATERAL * wet_west + jnp.maximum(u, 0.0)))
        cn = wet * (LATERAL * wet_north - jnp.minimum(v, 0.0))
        cs = wet * (LATERAL * wet_south + jnp.maximum(v, 0.0))
        coefs.append((1.0 - (ce + cw + cn + cs), ce, cw, cn, cs))
    mix = VERTICAL * wet

    def lateral(x, level, north, south):
        c0, ce, cw, cn, cs = coefs[level]
        return c0 * x + ce * shift(x, -1, 1) + cw * shift(x, 1, 1) + cn * north + cs * south

    for t in range(TRACERS):
        x = first[t * LEVELS : (t + 1) * LEVELS]
        y = []
        for level in range(LEVELS):
            k = t * LEVELS + level
            y.append(lateral(x[level], level, above(x[level], k), below(x[level], k)))
        d12, d23 = mix * (x[2] - x[1]), mix * (x[3] - x[2])
        for level, value in enumerate((y[0], y[1] + d12, y[2] + d23 - d12, y[3] - d23)):
            state_v[pl.ds((t * LEVELS + level) * ROWS, ROWS), :] = value

    c = lanes((COLS, 2 * COLS))
    slot_at = jnp.where(c < COLS, c // FLUX, (c - COLS) // FLUX + REACH * CAP)
    expand = jnp.where(slot_at == rows((COLS, 2 * COLS)), 1.0, 0.0).astype(BF16)
    target_row = jnp.dot(margin.astype(BF16), expand, preferred_element_type=F32)
    r, c = rows((FLUX * ROWS, 2 * COLS)), lanes((FLUX * ROWS, 2 * COLS))
    place = jnp.where(
        (target_row[0:1] == (r % ROWS).astype(F32)) & (c % FLUX == r // ROWS), 1.0, 0.0
    ).astype(BF16)

    for d in SENDS:
        @pl.when(late[d])
        def _():
            pl.semaphore_wait(ack_sem.at[place_of[d]], 1)
            if d in columns:
                columns[d].start()
            parts[d].start()

    for copy in columns.values():
        copy.wait_recv()
    from_west, from_east = col_in[0, 0:ROWS], col_in[1, 0:ROWS]
    from_both = jnp.where(lane % 2 == 1, from_west, from_east)

    def to_edge(x, k):
        return shift(x, -2 * k - 1, 1)

    wet_outside = to_edge(from_both, FIELDS)
    crossing = []
    for level in range(LEVELS):
        u = east_v[level]
        speed = jnp.where(at_east, -jnp.minimum(u, 0.0), jnp.maximum(u, 0.0))
        crossing.append(jnp.where(at_east | at_west, wet * (LATERAL * wet_outside + speed), 0.0))
    for k in range(FIELDS):
        where = pl.ds(k * ROWS, ROWS)
        state_v[where, :] = state_v[where, :] + crossing[k % LEVELS] * (to_edge(from_both, k) - first[k])
    for side, at in ((0, 0), (1, ROWS - 1)):
        row_out[1, side, FIELDS : FIELDS + 1, :] = from_west[at : at + 1]
        row_out[1, side, FIELDS + 1 : FIELDS + 2, :] = from_east[at : at + 1]
        for i, x in enumerate((from_west, from_east)):
            wet_corner = x[at : at + 1, 2 * FIELDS + 1 - i : 2 * FIELDS + 2 - i]
            row_out[1, side, FIELDS + 2 + i : FIELDS + 3 + i, :] = jnp.broadcast_to(wet_corner, (1, COLS))

    for d in OFFSETS:
        parts[d].wait_recv()
    arrived = [recv_v[g - REACH + SPAN, 0:DATA] for g in range(GROUPS)]
    arrived = jnp.concatenate(arrived[:SPAN] + [jnp.zeros((DATA, COLS), F32)] + arrived[SPAN:], axis=0)
    high, rest = split(arrived)
    ocean = jnp.dot(place, high, preferred_element_type=F32) + jnp.dot(place, rest, preferred_element_type=F32)
    ocean_o[...] = ocean
    q = ocean[(FLUX - 1) * ROWS :]
    top = wet * (0.05 + 0.15 * q * q / (1.0 + q * q))
    surface = [GAIN * wet * ocean[t * ROWS : (t + 1) * ROWS] for t in range(TRACERS)]
    for t in range(TRACERS):
        d01 = top * (first[t * LEVELS + 1] - first[t * LEVELS])
        for level, change in ((0, d01 + surface[t]), (1, -d01)):
            where = pl.ds((t * LEVELS + level) * ROWS, ROWS)
            state_v[where, :] = state_v[where, :] + change

    for side, at in ((0, 0), (1, ROWS - 1)):
        row_out[1, side, 0:FIELDS, :] = state_v[pl.ds(at, FIELDS, stride=ROWS), :]
    second_rows = row_copies(1)
    for d, copy in second_rows.items():
        @pl.when(there[d])
        def _():
            copy.start()

    level_of = (lane // 2) % LEVELS

    def beside(i):
        if i == 0:
            x, own, way, own_wet = from_west, to_west, 1, to_west[:, 2 * FIELDS : 2 * FIELDS + 1]
        else:
            x, own, way, own_wet = from_east, to_east, -1, to_east[:, 2 * FIELDS + 1 : 2 * FIELDS + 2]
        center = 2 * FIELDS + (1 - i)
        wet_c = jnp.broadcast_to(x[:, center : center + 1], (ROWS, COLS))
        wet_far = jnp.broadcast_to(x[:, center - way : center - way + 1], (ROWS, COLS))
        wet_own = jnp.broadcast_to(own_wet, (ROWS, COLS))

        def spread(at):
            moved = [shift(x, 2 * (t * LEVELS - at), 1) for t in range(TRACERS)]
            return jnp.where(lane < 2 * LEVELS, moved[0], jnp.where(lane < 4 * LEVELS, moved[1], moved[2]))

        u, v = spread(EAST_AT), spread(NORTH_AT)
        far, own = shift(x, way, 1), shift(own, way, 1)
        plus, minus = jnp.maximum(u, 0.0), -jnp.minimum(u, 0.0)
        c_far, c_own = (plus, minus) if i == 0 else (minus, plus)
        change = (LATERAL * wet_far + c_far) * (far - x) + (LATERAL * wet_own + c_own) * (own - x)
        step = shift(x, -2, 1) - x
        return x, wet_c, v, change, step

    halves = [beside(0), beside(1)]

    lists = jnp.where(edge_row == 0, col_in[0, ROWS:], col_in[1, ROWS:])
    target_row = jnp.dot(lists.astype(BF16), expand, preferred_element_type=F32)
    r = rows((ROWS, 2 * COLS)).astype(F32)
    on_row = [target_row[i : i + 1] == r for i in (0, 1)]
    c = lanes((2 * COLS, 2 * COLS))
    gather = jnp.where(
        rows((2 * COLS, 2 * COLS)) % FLUX == jnp.where(c < COLS, FLUX - 1, (c - COLS) // (2 * LEVELS)), 1.0, 0.0
    ).astype(BF16)
    quarter = lanes((8, COLS)) // DATA

    def along_lanes(base, at):
        out = [jnp.zeros((8, COLS), F32)] * 2
        for g in range(GROUPS):
            d = base + g
            ahead = d > 0 or (d == 0 and base != -2)
            value = recv_v[d + SPAN, DATA:] if d != 0 else edge_v[int(ahead)]
            out[ahead] = jnp.where(quarter == (g - REACH if ahead else g), value, out[ahead])
        return jnp.concatenate([tile[at : at + 1] for tile in out], axis=1)

    terms = [
        jnp.where(on_row[0], along_lanes(-2, 2), 0.0),
        jnp.where(on_row[1], along_lanes(-4, 0), 0.0),
    ]
    high, rest = split(jnp.concatenate(terms, axis=0))
    margins = jnp.dot(high, gather, preferred_element_type=F32) + jnp.dot(rest, gather, preferred_element_type=F32)
    inner = []
    for i, (x, wet_c, v, change, step) in enumerate(halves):
        q = margins[i * ROWS : (i + 1) * ROWS, 0:COLS]
        kv = 0.05 + 0.15 * q * q / (1.0 + q * q)
        face = jnp.where(level_of == LEVELS - 1, 0.0, jnp.where(level_of == 0, kv, VERTICAL) * step)
        source = jnp.where(level_of == 0, GAIN * margins[i * ROWS : (i + 1) * ROWS, COLS:], shift(-face, 2, 1))
        inner.append(change + face + source)

    for t in range(TRACERS):
        x = [state_v[pl.ds((t * LEVELS + level) * ROWS, ROWS), :] for level in range(LEVELS)]
        d01, d12, d23 = top * (x[1] - x[0]), mix * (x[2] - x[1]), mix * (x[3] - x[2])
        changes = (d01 + surface[t], d12 - d01, d23 - d12, -d23)
        for level, change in enumerate(changes):
            y = x[level]
            north = jnp.where(at_north, 0.0, shift(y, -1, 0))
            south = jnp.where(at_south, 0.0, shift(y, 1, 0))
            new_o[pl.ds((t * LEVELS + level) * ROWS, ROWS), :] = (
                lateral(y, level, north, south) - crossing[level] * y + change
            )

    halo, corner = [], []
    for i, ((x, wet_c, v, _, _), change) in enumerate(zip(halves, inner)):
        center = 2 * FIELDS + (1 - i)
        wet_n, wet_s = shift(wet_c, -1, 0), shift(wet_c, 1, 0)
        down_speed, up_speed = -jnp.minimum(v, 0.0), jnp.maximum(v, 0.0)
        north = jnp.where(at_north, 0.0, (LATERAL * wet_n + down_speed) * (shift(x, -1, 0) - x))
        south = jnp.where(at_south, 0.0, (LATERAL * wet_s + up_speed) * (shift(x, 1, 0) - x))
        halo.append(x + wet_c * (change + north + south))
        top_row, bottom_row = slice(ROWS - 1, ROWS), slice(0, 1)
        corner.append((
            (x[top_row], wet_c[top_row], down_speed[top_row]), (x[bottom_row], wet_c[bottom_row], up_speed[bottom_row])
        ))
    halo = jnp.where(lane % 2 == 1, halo[0], halo[1])
    row8 = rows((8, COLS))
    odd_lane = lanes((1, COLS)) % 2 == 1
    ends = []
    for level in range(LEVELS):
        _, _, _, cn, cs = coefs[level]
        cx = crossing[level]
        ends.append((
            jnp.where(row8 == 0, cx[0:8], 0.0), jnp.where(row8 == 7, cx[8:], 0.0),
            jnp.where(row8 == 0, cs[0:8], 0.0), jnp.where(row8 == 7, cn[8:], 0.0),
        ))
    for k in range(FIELDS):
        where = pl.ds(k * ROWS, ROWS)
        new_o[where, :] = new_o[where, :] + crossing[k % LEVELS] * to_edge(halo, k)

    for copy in (*parts.values(), *columns.values()):
        copy.wait_send()
    of_rows(first_rows, "send")
    of_rows(second_rows, "recv")
    north_rows, south_rows = edges(1)
    lift = []
    for side, beyond in ((0, north_rows), (1, south_rows)):
        each = []
        for i in range(2):
            x, wet_c, speed = corner[i][side]
            there_x = beyond[FIELDS + i : FIELDS + i + 1]
            there_wet = beyond[FIELDS + 2 + i : FIELDS + 3 + i]
            each.append(wet_c * (LATERAL * there_wet + speed) * (there_x - x))
        lift.append(jnp.where(odd_lane, each[0], each[1]))
    lift = jnp.where(row8 == 7, lift[0], lift[1])
    for k in range(FIELDS):
        x_low, x_high, c_low, c_high = ends[k % LEVELS]
        low, high = pl.ds(k * ROWS, 8), pl.ds(k * ROWS + 8, 8)
        moved = to_edge(lift, k)
        new_o[low, :] = new_o[low, :] + x_low * moved + c_low * south_rows[k : k + 1]
        new_o[high, :] = new_o[high, :] + x_high * moved + c_high * north_rows[k : k + 1]

    of_rows(second_rows, "send")


def store(ocean_v, new_v, ocean_o, new_o, sem):
    copies = [
        pltpu.make_async_copy(new_v, new_o, sem.at[0]),
        pltpu.make_async_copy(ocean_v, ocean_o, sem.at[1]),
    ]
    for copy in copies:
        copy.start()
    for copy in copies:
        copy.wait()


def body(
    atm_flux, remap_weight, source_block, send_counts, recv_rows, land_mask, tracers, east_velocity, north_velocity
):
    hbm = pl.BlockSpec(memory_space=pltpu.HBM)
    vmem = pl.BlockSpec(memory_space=pltpu.VMEM)
    ocean, new = pl.pallas_call(
        kernel,
        out_shape=(
            jax.ShapeDtypeStruct((FLUX * ROWS, COLS), F32),
            jax.ShapeDtypeStruct((FIELDS * ROWS, COLS), F32),
        ),
        in_specs=[hbm] * 9,
        out_specs=(vmem, vmem),
        scratch_shapes=[
            pltpu.VMEM((FLUX, BLOCKS * COLS), BF16),
            pltpu.VMEM((SLOTS, COLS, COLS), BF16),
            pltpu.VMEM((1, SLOTS), jnp.int32),
            pltpu.VMEM((1, GROUPS), jnp.int32),
            pltpu.VMEM((1, SLOTS), jnp.int32),
            pltpu.VMEM((ROWS, COLS), jnp.int32),
            pltpu.VMEM((FIELDS * ROWS, COLS), F32),
            pltpu.VMEM((LEVELS, ROWS, COLS), F32),
            pltpu.VMEM((LEVELS, ROWS, COLS), F32),
            pltpu.VMEM((FLUX * SLOTS, 2 * COLS), BF16),
            pltpu.VMEM((FLUX * SLOTS, COLS), F32),
            pltpu.VMEM((2, 8, COLS), F32),
            pltpu.VMEM((GROUPS, DATA + 8, COLS), F32),
            pltpu.VMEM((2 * SPAN + 1, DATA + 8, COLS), F32),
            pltpu.VMEM((FIELDS * ROWS, COLS), F32),
            pltpu.VMEM((2, ROWS + 8, COLS), F32),
            pltpu.VMEM((2, ROWS + 8, COLS), F32),
            pltpu.VMEM((2, 2, ROWS, COLS), F32),
            pltpu.VMEM((2, 2, ROWS, COLS), F32),
            pltpu.SemaphoreType.DMA((8,)),
            pltpu.SemaphoreType.DMA((GROUPS,)),
            pltpu.SemaphoreType.DMA((2 * SPAN + 1,)),
            pltpu.SemaphoreType.DMA((2 * SPAN + 1,)),
            pltpu.SemaphoreType.DMA((3, 2)),
            pltpu.SemaphoreType.DMA((3, 2)),
            pltpu.SemaphoreType.REGULAR((len(OFFSETS) + 2,)),
        ],
        compiler_params=pltpu.CompilerParams(
            collective_id=0, has_side_effects=True, vmem_limit_bytes=32 * 1024 * 1024
        ),
    )(*(pltpu.with_memory_space_constraint(a, pltpu.HBM) for a in (
        atm_flux.reshape(FLUX, BLOCKS * COLS),
        remap_weight.reshape(SLOTS, COLS, COLS),
        source_block,
        send_counts,
        recv_rows,
        land_mask,
        tracers.reshape(FIELDS * ROWS, COLS),
        east_velocity,
        north_velocity,
    )))
    ocean, new = pl.pallas_call(
        store,
        out_shape=(
            jax.ShapeDtypeStruct((FLUX * ROWS, COLS), F32),
            jax.ShapeDtypeStruct((FIELDS * ROWS, COLS), F32),
        ),
        in_specs=[vmem, vmem],
        out_specs=(hbm, hbm),
        scratch_shapes=[pltpu.SemaphoreType.DMA((2,))],
    )(*(pltpu.with_memory_space_constraint(a, pltpu.VMEM) for a in (ocean, new)))
    return (ocean.reshape(FLUX, ROWS, COLS), new.reshape(TRACERS, LEVELS, ROWS, COLS))


def solution(mesh):
    in_specs = (
        P(None, "oy", "ox"),
        P("oy", "ox", None, None),
        P("oy", "ox"),
        P("oy", "ox"),
        P("oy", "ox"),
        P("oy", "ox"),
        P(None, None, "oy", "ox"),
        P(None, "oy", "ox"),
        P(None, "oy", "ox"),
    )
    out_specs = (P(None, "oy", "ox"), P(None, None, "oy", "ox"))
    return jax.shard_map(body, mesh=mesh, in_specs=in_specs, out_specs=out_specs, check_vma=False)
```

```python
import jax
import jax.numpy as jnp
from jax import lax
from jax.experimental import pallas as pl
from jax.experimental.pallas import tpu as pltpu
from jax.sharding import PartitionSpec as P

MESH = pl.DeviceIdType.MESH
FLUX = 4
TRACERS = 3
LEVELS = 4
FIELDS = TRACERS * LEVELS
ROWS = 16
COLS = 128
BLOCKS = 6
REACH = 3
CAP = 8
GROUPS = 7
SLOTS = GROUPS * CAP
RING = 8
SPAN = REACH + 1
OFFSETS = (-4, -3, -2, -1, 1, 2, 3, 4)
SENDS = (1, 2, 3, 4, -4, -3, -2, -1)
DATA = 32
AHEAD = (6, 5, 4, 3)
BEHIND = (0, 1, 2)
EAST_AT = 16
NORTH_AT = 20
LATERAL = 0.08
VERTICAL = 0.1
GAIN = 0.5
F32 = jnp.float32
BF16 = jnp.bfloat16


def lanes(shape):
    return lax.broadcasted_iota(jnp.int32, shape, len(shape) - 1)


def rows(shape):
    return lax.broadcasted_iota(jnp.int32, shape, len(shape) - 2)


def kernel(
    flux_h, weight_h, source_h, count_h, recv_h, land_h, tracer_h, east_h, north_h,
    ocean_o, new_o,
    flux_v, weight_v, source_v, count_v, place_v, land_v, tracer_v, east_v, north_v,
    lhs_v, part_v, edge_v, send_v, recv_v, state_v, col_out, col_in, row_out, row_in,
    load_sem, weight_sem, part_send, part_recv, halo_send, halo_recv, ack_sem,
):
    oy, ox = lax.axis_index("oy"), lax.axis_index("ox")
    n_oy, n_ox = lax.axis_size("oy"), lax.axis_size("ox")

    def along(offset):
        return (oy, lax.rem(ox + (n_ox + offset), n_ox))

    up = (lax.rem(oy + 1, n_oy), ox)
    down = (lax.rem(oy + (n_oy - 1), n_oy), ox)

    loads = {}
    for i, (name, src, dst) in enumerate((
        ("tracer", tracer_h, tracer_v), ("land", land_h, land_v), ("flux", flux_h, flux_v),
        ("source", source_h, source_v), ("count", count_h, count_v), ("place", recv_h, place_v),
        ("east", east_h, east_v), ("north", north_h, north_v),
    )):
        loads[name] = pltpu.make_async_copy(src, dst, load_sem.at[i])
    weights = {}
    for i, groups in enumerate((AHEAD, BEHIND)):
        span = pl.ds(min(groups) * CAP, len(groups) * CAP)
        weights[groups] = pltpu.make_async_copy(weight_h.at[span], weight_v.at[span], weight_sem.at[i])
    for name in ("flux", "source", "count", "tracer", "land", "place", "east", "north"):
        loads[name].start()
    for copy in weights.values():
        copy.start()

    key = lax.rem(ox, RING)
    odd = lax.rem(oy, 2)
    partners = {"up": up, "down": down} | {d: along(d) for d in OFFSETS}
    later = {d: lax.rem(key + (d + RING), RING) > key for d in OFFSETS}
    later["up"] = later["down"] = odd == 1
    there = {"up": oy != n_oy - 1, "down": oy != 0}
    late = {d: later[d] & there[d] if d in there else later[d] for d in partners}
    early = {d: jnp.logical_not(later[d]) & there[d] if d in there else jnp.logical_not(later[d]) for d in partners}
    opposite = {d: -d for d in OFFSETS} | {"up": "down", "down": "up"}
    place_of = {d: i for i, d in enumerate(partners)}
    barrier = pltpu.get_barrier_semaphore()
    announced = jnp.int32(0)
    for d in partners:
        announced += jnp.where(early[d], 1, 0)

        @pl.when(late[d])
        def _():
            pl.semaphore_signal(barrier, inc=1, device_id=partners[d], device_id_type=MESH)

    def remote(src, dst, send, recv, device):
        return pltpu.make_async_remote_copy(
            src_ref=src, dst_ref=dst, send_sem=send, recv_sem=recv, device_id=device, device_id_type=MESH
        )

    def row_copies(e):
        return {
            "down": remote(row_out.at[e, 0], row_in.at[e, 0], halo_send.at[e, 0], halo_recv.at[e, 0], down),
            "up": remote(row_out.at[e, 1], row_in.at[e, 1], halo_send.at[e, 1], halo_recv.at[e, 1], up),
        }

    first_rows = row_copies(0)
    columns = {
        1: remote(col_out.at[0], col_in.at[0], halo_send.at[2, 0], halo_recv.at[2, 0], partners[1]),
        -1: remote(col_out.at[1], col_in.at[1], halo_send.at[2, 1], halo_recv.at[2, 1], partners[-1]),
    }
    parts = {}
    for d in OFFSETS:
        if abs(d) <= REACH:
            src, dst = send_v.at[d + REACH], recv_v.at[d + SPAN]
        else:
            src, dst = edge_v.at[int(d > 0)], recv_v.at[d + SPAN, pl.ds(DATA, 8)]
        parts[d] = remote(src, dst, part_send.at[d + SPAN], part_recv.at[d + SPAN], partners[d])

    lane = lanes((ROWS, COLS))
    row = rows((ROWS, COLS))

    def shift(x, by, axis):
        return pltpu.roll(x, by % x.shape[axis], axis)

    for name in ("flux", "source", "count"):
        loads[name].wait()
    flux = flux_v[...].astype(F32)
    blocks = jnp.concatenate([flux[:, n * COLS : (n + 1) * COLS] for n in range(BLOCKS)], axis=0)
    blocks = jnp.concatenate([blocks, jnp.zeros((COLS - FLUX * BLOCKS, COLS), F32)], axis=0).astype(BF16)

    def left(groups):
        start, wide = min(groups) * DATA, len(groups) * DATA
        at_slot = (rows((wide, SLOTS)) + start) // FLUX == lanes((wide, SLOTS))
        at_group = (rows((wide, GROUPS)) + start) // DATA == lanes((wide, GROUPS))
        source = jnp.where(at_slot, source_v[...].astype(F32), 0.0).astype(BF16)
        count = jnp.where(at_group, count_v[...].astype(F32), 0.0).astype(BF16)
        source = jnp.dot(source, jnp.ones((SLOTS, COLS), BF16), preferred_element_type=F32)
        count = jnp.dot(count, jnp.ones((GROUPS, COLS), BF16), preferred_element_type=F32)
        r, c = rows((wide, COLS)), lanes((wide, COLS))
        pick = (
            (source == (c // FLUX).astype(F32))
            & (r % FLUX == c % FLUX)
            & (((r // FLUX) % CAP).astype(F32) < count)
        )
        chosen = jnp.dot(jnp.where(pick, 1.0, 0.0).astype(BF16), blocks, preferred_element_type=F32)
        low = r % 16 < 8
        lhs_v[pl.ds(start, wide), 0:COLS] = jnp.where(low, chosen, 0.0).astype(BF16)
        lhs_v[pl.ds(start, wide), COLS : 2 * COLS] = jnp.where(low, 0.0, chosen).astype(BF16)

    wide = FLUX * SLOTS

    half = rows((16, COLS)) % 8 < 4
    edge_row = rows((8, COLS))
    ends = jnp.where(lanes((8, COLS)) == jnp.where(edge_row < 2, 0, COLS - 1), 1.0, 0.0).astype(BF16)
    dims = (((1,), (1,)), ((), ()))

    def split(x):
        high = x.astype(BF16)
        return high, (x - high.astype(F32)).astype(BF16)

    def remap(groups):
        for g in groups:
            for q in (2 * g, 2 * g + 1):
                w = [weight_v[4 * q + j] for j in range(4)]
                tile = jnp.concatenate(
                    [jnp.concatenate(w[0:2], axis=1), jnp.concatenate(w[2:4], axis=1)], axis=0
                )
                both = jnp.dot(lhs_v[pl.ds(16 * q, 16), :], tile, preferred_element_type=F32)
                value = jnp.where(half, both[:, 0:COLS], both[:, COLS:])
                part_v[pl.ds(16 * q, 16), :] = value
                if g == REACH:
                    recv_v[SPAN, pl.ds(16 * (q - 2 * g), 16), :] = value
                else:
                    send_v[g, pl.ds(16 * (q - 2 * g), 16), :] = value

    def edge_columns(base, groups, at):
        high, rest = split(part_v[pl.ds(base * DATA, COLS), :])
        edge = lax.dot_general(ends, high, dims, preferred_element_type=F32)
        edge = edge + lax.dot_general(ends, rest, dims, preferred_element_type=F32)
        for g in groups:
            send_v[g, DATA:, :] = edge
        edge_v[at] = edge

    left(AHEAD)
    weights[AHEAD].wait()
    for name in ("tracer", "land", "place", "east", "north"):
        loads[name].wait()
    wet = land_v[...].astype(F32)
    first = [tracer_v[pl.ds(k * ROWS, ROWS), :] for k in range(FIELDS)]
    for side, at in ((0, 0), (1, ROWS - 1)):
        row_out[0, side, 0:FIELDS, :] = tracer_v[pl.ds(at, FIELDS, stride=ROWS), :]
        row_out[0, side, FIELDS:ROWS, :] = jnp.broadcast_to(wet[at : at + 1], (ROWS - FIELDS, COLS))
    packed = {k: first[k] for k in range(FIELDS)} | {FIELDS: wet}
    packed |= {EAST_AT + k: east_v[k] for k in range(LEVELS)} | {NORTH_AT + k: north_v[k] for k in range(LEVELS)}
    to_east = jnp.zeros((ROWS, COLS), F32)
    to_west = jnp.zeros((ROWS, COLS), F32)
    for k, field in packed.items():
        to_east = jnp.where(lane // 2 == k, shift(field, 2 * k + 2, 1), to_east)
        to_west = jnp.where(lane // 2 == k, shift(field, 2 * k, 1), to_west)
    margin = jnp.broadcast_to(place_v[...].astype(F32), (8, SLOTS)).astype(BF16)
    same = jnp.where(lanes((SLOTS, COLS)) == rows((SLOTS, COLS)), 1.0, 0.0).astype(BF16)
    margin = jnp.dot(margin, same, preferred_element_type=F32)
    for i, value in enumerate((to_east, to_west)):
        col_out[i, 0:ROWS, :] = value
        col_out[i, ROWS:, :] = margin

    remap(AHEAD)
    edge_columns(REACH, AHEAD[:-1], 1)

    @pl.when(announced > 0)
    def _():
        pl.semaphore_wait(barrier, announced)

    for d in partners:
        @pl.when(early[d])
        def _():
            pl.semaphore_signal(
                ack_sem.at[place_of[opposite[d]]], inc=1, device_id=partners[d], device_id_type=MESH
            )

    @pl.when(early[1])
    def _():
        columns[1].start()

    for d in SENDS[0:SPAN]:
        @pl.when(early[d])
        def _():
            parts[d].start()

    left(BEHIND)
    weights[BEHIND].wait()
    remap(BEHIND)
    edge_columns(0, BEHIND, 0)

    for d in SENDS[SPAN:]:
        @pl.when(early[d])
        def _():
            parts[d].start()
    for d, copy in (("up", first_rows["up"]), ("down", first_rows["down"]), (-1, columns[-1])):
        @pl.when(early[d])
        def _():
            copy.start()
    for d in ("up", "down"):
        @pl.when(late[d])
        def _():
            pl.semaphore_wait(ack_sem.at[place_of[d]], 1)
            first_rows[d].start()
    def edges(e):
        north_rows, south_rows = row_in[e, 0], row_in[e, 1]
        north_rows = jnp.where(oy == n_oy - 1, 0.0, north_rows)
        south_rows = jnp.where(oy == 0, 0.0, south_rows)
        return north_rows, south_rows

    def of_rows(copies, wait):
        for d, copy in copies.items():
            @pl.when(there[d if wait == "send" else opposite[d]])
            def _():
                copy.wait_send() if wait == "send" else copy.wait_recv()

    of_rows(first_rows, "recv")
    at_east, at_west = lane == COLS - 1, lane == 0
    at_north, at_south = row == ROWS - 1, row == 0
    north_rows, south_rows = edges(0)

    def above(x, k):
        return jnp.where(at_north, north_rows[k : k + 1], shift(x, -1, 0))

    def below(x, k):
        return jnp.where(at_south, south_rows[k : k + 1], shift(x, 1, 0))

    wet_east, wet_west = shift(wet, -1, 1), shift(wet, 1, 1)
    wet_north, wet_south = above(wet, FIELDS), below(wet, FIELDS)
    coefs = []
    for level in range(LEVELS):
        u, v = east_v[level], north_v[level]
        ce = jnp.where(at_east, 0.0, wet * (LATERAL * wet_east - jnp.minimum(u, 0.0)))
        cw = jnp.where(at_west, 0.0, wet * (LATERAL * wet_west + jnp.maximum(u, 0.0)))
        cn = wet * (LATERAL * wet_north - jnp.minimum(v, 0.0))
        cs = wet * (LATERAL * wet_south + jnp.maximum(v, 0.0))
        coefs.append((1.0 - (ce + cw + cn + cs), ce, cw, cn, cs))
    mix = VERTICAL * wet

    def lateral(x, level, north, south):
        c0, ce, cw, cn, cs = coefs[level]
        return c0 * x + ce * shift(x, -1, 1) + cw * shift(x, 1, 1) + cn * north + cs * south

    for t in range(TRACERS):
        x = first[t * LEVELS : (t + 1) * LEVELS]
        y = []
        for level in range(LEVELS):
            k = t * LEVELS + level
            y.append(lateral(x[level], level, above(x[level], k), below(x[level], k)))
        d12, d23 = mix * (x[2] - x[1]), mix * (x[3] - x[2])
        for level, value in enumerate((y[0], y[1] + d12, y[2] + d23 - d12, y[3] - d23)):
            state_v[pl.ds((t * LEVELS + level) * ROWS, ROWS), :] = value

    c = lanes((COLS, 2 * COLS))
    slot_at = jnp.where(c < COLS, c // FLUX, (c - COLS) // FLUX + REACH * CAP)
    expand = jnp.where(slot_at == rows((COLS, 2 * COLS)), 1.0, 0.0).astype(BF16)
    target_row = jnp.dot(margin.astype(BF16), expand, preferred_element_type=F32)
    r, c = rows((FLUX * ROWS, 2 * COLS)), lanes((FLUX * ROWS, 2 * COLS))
    place = jnp.where(
        (target_row[0:1] == (r % ROWS).astype(F32)) & (c % FLUX == r // ROWS), 1.0, 0.0
    ).astype(BF16)

    for d in SENDS:
        @pl.when(late[d])
        def _():
            pl.semaphore_wait(ack_sem.at[place_of[d]], 1)
            if d in columns:
                columns[d].start()
            parts[d].start()

    for copy in columns.values():
        copy.wait_recv()
    from_west, from_east = col_in[0, 0:ROWS], col_in[1, 0:ROWS]
    from_both = jnp.where(lane % 2 == 1, from_west, from_east)

    def to_edge(x, k):
        return shift(x, -2 * k - 1, 1)

    wet_outside = to_edge(from_both, FIELDS)
    crossing = []
    for level in range(LEVELS):
        u = east_v[level]
        speed = jnp.where(at_east, -jnp.minimum(u, 0.0), jnp.maximum(u, 0.0))
        crossing.append(jnp.where(at_east | at_west, wet * (LATERAL * wet_outside + speed), 0.0))
    for k in range(FIELDS):
        where = pl.ds(k * ROWS, ROWS)
        state_v[where, :] = state_v[where, :] + crossing[k % LEVELS] * (to_edge(from_both, k) - first[k])
    for side, at in ((0, 0), (1, ROWS - 1)):
        row_out[1, side, FIELDS : FIELDS + 1, :] = from_west[at : at + 1]
        row_out[1, side, FIELDS + 1 : FIELDS + 2, :] = from_east[at : at + 1]
        for i, x in enumerate((from_west, from_east)):
            wet_corner = x[at : at + 1, 2 * FIELDS + 1 - i : 2 * FIELDS + 2 - i]
            row_out[1, side, FIELDS + 2 + i : FIELDS + 3 + i, :] = jnp.broadcast_to(wet_corner, (1, COLS))

    for d in OFFSETS:
        parts[d].wait_recv()
    arrived = [recv_v[g - REACH + SPAN, 0:DATA] for g in range(GROUPS)]
    arrived = jnp.concatenate(arrived[:SPAN] + [jnp.zeros((DATA, COLS), F32)] + arrived[SPAN:], axis=0)
    high, rest = split(arrived)
    ocean = jnp.dot(place, high, preferred_element_type=F32) + jnp.dot(place, rest, preferred_element_type=F32)
    ocean_o[...] = ocean
    q = ocean[(FLUX - 1) * ROWS :]
    top = wet * (0.05 + 0.15 * q * q / (1.0 + q * q))
    surface = [GAIN * wet * ocean[t * ROWS : (t + 1) * ROWS] for t in range(TRACERS)]
    for t in range(TRACERS):
        d01 = top * (first[t * LEVELS + 1] - first[t * LEVELS])
        for level, change in ((0, d01 + surface[t]), (1, -d01)):
            where = pl.ds((t * LEVELS + level) * ROWS, ROWS)
            state_v[where, :] = state_v[where, :] + change

    for side, at in ((0, 0), (1, ROWS - 1)):
        row_out[1, side, 0:FIELDS, :] = state_v[pl.ds(at, FIELDS, stride=ROWS), :]
    second_rows = row_copies(1)
    for d, copy in second_rows.items():
        @pl.when(there[d])
        def _():
            copy.start()

    level_of = (lane // 2) % LEVELS

    def beside(i):
        if i == 0:
            x, own, way, own_wet = from_west, to_west, 1, to_west[:, 2 * FIELDS : 2 * FIELDS + 1]
        else:
            x, own, way, own_wet = from_east, to_east, -1, to_east[:, 2 * FIELDS + 1 : 2 * FIELDS + 2]
        center = 2 * FIELDS + (1 - i)
        wet_c = jnp.broadcast_to(x[:, center : center + 1], (ROWS, COLS))
        wet_far = jnp.broadcast_to(x[:, center - way : center - way + 1], (ROWS, COLS))
        wet_own = jnp.broadcast_to(own_wet, (ROWS, COLS))

        def spread(at):
            moved = [shift(x, 2 * (t * LEVELS - at), 1) for t in range(TRACERS)]
            return jnp.where(lane < 2 * LEVELS, moved[0], jnp.where(lane < 4 * LEVELS, moved[1], moved[2]))

        u, v = spread(EAST_AT), spread(NORTH_AT)
        far, own = shift(x, way, 1), shift(own, way, 1)
        plus, minus = jnp.maximum(u, 0.0), -jnp.minimum(u, 0.0)
        c_far, c_own = (plus, minus) if i == 0 else (minus, plus)
        change = (LATERAL * wet_far + c_far) * (far - x) + (LATERAL * wet_own + c_own) * (own - x)
        step = shift(x, -2, 1) - x
        return x, wet_c, v, change, step

    halves = [beside(0), beside(1)]

    lists = jnp.where(edge_row == 0, col_in[0, ROWS:], col_in[1, ROWS:])
    target_row = jnp.dot(lists.astype(BF16), expand, preferred_element_type=F32)
    r = rows((ROWS, 2 * COLS)).astype(F32)
    on_row = [target_row[i : i + 1] == r for i in (0, 1)]
    c = lanes((2 * COLS, 2 * COLS))
    gather = jnp.where(
        rows((2 * COLS, 2 * COLS)) % FLUX == jnp.where(c < COLS, FLUX - 1, (c - COLS) // (2 * LEVELS)), 1.0, 0.0
    ).astype(BF16)
    quarter = lanes((8, COLS)) // DATA

    def along_lanes(base, at):
        out = [jnp.zeros((8, COLS), F32)] * 2
        for g in range(GROUPS):
            d = base + g
            ahead = d > 0 or (d == 0 and base != -2)
            value = recv_v[d + SPAN, DATA:] if d != 0 else edge_v[int(ahead)]
            out[ahead] = jnp.where(quarter == (g - REACH if ahead else g), value, out[ahead])
        return jnp.concatenate([tile[at : at + 1] for tile in out], axis=1)

    terms = [
        jnp.where(on_row[0], along_lanes(-2, 2), 0.0),
        jnp.where(on_row[1], along_lanes(-4, 0), 0.0),
    ]
    high, rest = split(jnp.concatenate(terms, axis=0))
    margins = jnp.dot(high, gather, preferred_element_type=F32) + jnp.dot(rest, gather, preferred_element_type=F32)
    inner = []
    for i, (x, wet_c, v, change, step) in enumerate(halves):
        q = margins[i * ROWS : (i + 1) * ROWS, 0:COLS]
        kv = 0.05 + 0.15 * q * q / (1.0 + q * q)
        face = jnp.where(level_of == LEVELS - 1, 0.0, jnp.where(level_of == 0, kv, VERTICAL) * step)
        source = jnp.where(level_of == 0, GAIN * margins[i * ROWS : (i + 1) * ROWS, COLS:], shift(-face, 2, 1))
        inner.append(change + face + source)

    for t in range(TRACERS):
        x = [state_v[pl.ds((t * LEVELS + level) * ROWS, ROWS), :] for level in range(LEVELS)]
        d01, d12, d23 = top * (x[1] - x[0]), mix * (x[2] - x[1]), mix * (x[3] - x[2])
        changes = (d01 + surface[t], d12 - d01, d23 - d12, -d23)
        for level, change in enumerate(changes):
            y = x[level]
            north = jnp.where(at_north, 0.0, shift(y, -1, 0))
            south = jnp.where(at_south, 0.0, shift(y, 1, 0))
            new_o[pl.ds((t * LEVELS + level) * ROWS, ROWS), :] = (
                lateral(y, level, north, south) - crossing[level] * y + change
            )

    halo, corner = [], []
    for i, ((x, wet_c, v, _, _), change) in enumerate(zip(halves, inner)):
        center = 2 * FIELDS + (1 - i)
        wet_n, wet_s = shift(wet_c, -1, 0), shift(wet_c, 1, 0)
        down_speed, up_speed = -jnp.minimum(v, 0.0), jnp.maximum(v, 0.0)
        north = jnp.where(at_north, 0.0, (LATERAL * wet_n + down_speed) * (shift(x, -1, 0) - x))
        south = jnp.where(at_south, 0.0, (LATERAL * wet_s + up_speed) * (shift(x, 1, 0) - x))
        halo.append(x + wet_c * (change + north + south))
        top_row, bottom_row = slice(ROWS - 1, ROWS), slice(0, 1)
        corner.append((
            (x[top_row], wet_c[top_row], down_speed[top_row]), (x[bottom_row], wet_c[bottom_row], up_speed[bottom_row])
        ))
    halo = jnp.where(lane % 2 == 1, halo[0], halo[1])
    row8 = rows((8, COLS))
    odd_lane = lanes((1, COLS)) % 2 == 1
    ends = []
    for level in range(LEVELS):
        _, _, _, cn, cs = coefs[level]
        cx = crossing[level]
        ends.append((
            jnp.where(row8 == 0, cx[0:8], 0.0), jnp.where(row8 == 7, cx[8:], 0.0),
            jnp.where(row8 == 0, cs[0:8], 0.0), jnp.where(row8 == 7, cn[8:], 0.0),
        ))
    for k in range(FIELDS):
        where = pl.ds(k * ROWS, ROWS)
        new_o[where, :] = new_o[where, :] + crossing[k % LEVELS] * to_edge(halo, k)

    for copy in (*parts.values(), *columns.values()):
        copy.wait_send()
    of_rows(first_rows, "send")
    of_rows(second_rows, "recv")
    north_rows, south_rows = edges(1)
    lift = []
    for side, beyond in ((0, north_rows), (1, south_rows)):
        each = []
        for i in range(2):
            x, wet_c, speed = corner[i][side]
            there_x = beyond[FIELDS + i : FIELDS + i + 1]
            there_wet = beyond[FIELDS + 2 + i : FIELDS + 3 + i]
            each.append(wet_c * (LATERAL * there_wet + speed) * (there_x - x))
        lift.append(jnp.where(odd_lane, each[0], each[1]))
    lift = jnp.where(row8 == 7, lift[0], lift[1])
    for k in range(FIELDS):
        x_low, x_high, c_low, c_high = ends[k % LEVELS]
        low, high = pl.ds(k * ROWS, 8), pl.ds(k * ROWS + 8, 8)
        moved = to_edge(lift, k)
        new_o[low, :] = new_o[low, :] + x_low * moved + c_low * south_rows[k : k + 1]
        new_o[high, :] = new_o[high, :] + x_high * moved + c_high * north_rows[k : k + 1]

    of_rows(second_rows, "send")


def store(ocean_v, new_v, ocean_o, new_o, sem):
    copies = [
        pltpu.make_async_copy(new_v, new_o, sem.at[0]),
        pltpu.make_async_copy(ocean_v, ocean_o, sem.at[1]),
    ]
    for copy in copies:
        copy.start()
    for copy in copies:
        copy.wait()


def body(
    atm_flux, remap_weight, source_block, send_counts, recv_rows, land_mask, tracers, east_velocity, north_velocity
):
    hbm = pl.BlockSpec(memory_space=pltpu.HBM)
    vmem = pl.BlockSpec(memory_space=pltpu.VMEM)
    ocean, new = pl.pallas_call(
        kernel,
        out_shape=(
            jax.ShapeDtypeStruct((FLUX * ROWS, COLS), F32),
            jax.ShapeDtypeStruct((FIELDS * ROWS, COLS), F32),
        ),
        in_specs=[hbm] * 9,
        out_specs=(vmem, vmem),
        scratch_shapes=[
            pltpu.VMEM((FLUX, BLOCKS * COLS), BF16),
            pltpu.VMEM((SLOTS, COLS, COLS), BF16),
            pltpu.VMEM((1, SLOTS), jnp.int32),
            pltpu.VMEM((1, GROUPS), jnp.int32),
            pltpu.VMEM((1, SLOTS), jnp.int32),
            pltpu.VMEM((ROWS, COLS), jnp.int32),
            pltpu.VMEM((FIELDS * ROWS, COLS), F32),
            pltpu.VMEM((LEVELS, ROWS, COLS), F32),
            pltpu.VMEM((LEVELS, ROWS, COLS), F32),
            pltpu.VMEM((FLUX * SLOTS, 2 * COLS), BF16),
            pltpu.VMEM((FLUX * SLOTS, COLS), F32),
            pltpu.VMEM((2, 8, COLS), F32),
            pltpu.VMEM((GROUPS, DATA + 8, COLS), F32),
            pltpu.VMEM((2 * SPAN + 1, DATA + 8, COLS), F32),
            pltpu.VMEM((FIELDS * ROWS, COLS), F32),
            pltpu.VMEM((2, ROWS + 8, COLS), F32),
            pltpu.VMEM((2, ROWS + 8, COLS), F32),
            pltpu.VMEM((2, 2, ROWS, COLS), F32),
            pltpu.VMEM((2, 2, ROWS, COLS), F32),
            pltpu.SemaphoreType.DMA((8,)),
            pltpu.SemaphoreType.DMA((GROUPS,)),
            pltpu.SemaphoreType.DMA((2 * SPAN + 1,)),
            pltpu.SemaphoreType.DMA((2 * SPAN + 1,)),
            pltpu.SemaphoreType.DMA((3, 2)),
            pltpu.SemaphoreType.DMA((3, 2)),
            pltpu.SemaphoreType.REGULAR((len(OFFSETS) + 2,)),
        ],
        compiler_params=pltpu.CompilerParams(
            collective_id=0, has_side_effects=True, vmem_limit_bytes=32 * 1024 * 1024
        ),
    )(*(pltpu.with_memory_space_constraint(a, pltpu.HBM) for a in (
        atm_flux.reshape(FLUX, BLOCKS * COLS),
        remap_weight.reshape(SLOTS, COLS, COLS),
        source_block,
        send_counts,
        recv_rows,
        land_mask,
        tracers.reshape(FIELDS * ROWS, COLS),
        east_velocity,
        north_velocity,
    )))
    ocean, new = pl.pallas_call(
        store,
        out_shape=(
            jax.ShapeDtypeStruct((FLUX * ROWS, COLS), F32),
            jax.ShapeDtypeStruct((FIELDS * ROWS, COLS), F32),
        ),
        in_specs=[vmem, vmem],
        out_specs=(hbm, hbm),
        scratch_shapes=[pltpu.SemaphoreType.DMA((2,))],
    )(*(pltpu.with_memory_space_constraint(a, pltpu.VMEM) for a in (ocean, new)))
    return (ocean.reshape(FLUX, ROWS, COLS), new.reshape(TRACERS, LEVELS, ROWS, COLS))


def solution(mesh):
    in_specs = (
        P(None, "oy", "ox"),
        P("oy", "ox", None, None),
        P("oy", "ox"),
        P("oy", "ox"),
        P("oy", "ox"),
        P("oy", "ox"),
        P(None, None, "oy", "ox"),
        P(None, "oy", "ox"),
        P(None, "oy", "ox"),
    )
    out_specs = (P(None, "oy", "ox"), P(None, None, "oy", "ox"))
    return jax.shard_map(body, mesh=mesh, in_specs=in_specs, out_specs=out_specs, check_vma=False)
```
